32 devices in a mesh: replica: 4 (over x, core), shard: 8 (over z, y).
Axes of the slice: x: 2, y: 2, z: 4, core: 2. Of those that a mesh axis runs over, the one named last changes fastest.
Arguments:
- tokens: bfloat16 [4096, 768], P(('replica', 'shard')), may hold values from -6 to 6
- lengths: int32 [32, 4], P(('replica', 'shard')), may hold values from 0 to 128, as said below
- qkv_weight: bfloat16 [768, 2304], P('shard'), may hold values from -0.21875 to 0.21875
- qv_bias: bfloat16 [1536], P('shard'), may hold values from -3 to 3
- out_weight: bfloat16 [768, 768], P('shard'), may hold values from -0.875 to 0.875
- out_bias: bfloat16 [768], P('shard'), may hold values from -2 to 2
- first_gain: bfloat16 [768], P('shard'), may hold values from 0.5 to 1.5
- first_shift: bfloat16 [768], P('shard'), may hold values from -2 to 2
- up_weight: bfloat16 [768, 3072], P('shard'), may hold values from -0.21875 to 0.21875
- up_bias: bfloat16 [3072], P('shard'), may hold values from -3 to 3
- down_weight: bfloat16 [3072, 768], P('shard'), may hold values from -0.109375 to 0.109375
- down_bias: bfloat16 [768], P('shard'), may hold values from -2 to 2
- second_gain: bfloat16 [768], P('shard'), may hold values from 0.5 to 1.5
- second_shift: bfloat16 [768], P('shard'), may hold values from -2 to 2
- cotangent: bfloat16 [4096, 768], P(('replica', 'shard')), may hold values from -6 to 6
Outputs:
- layer_out: bfloat16 [4096, 768], P(('replica', 'shard'))
- grad_tokens: bfloat16 [4096, 768], P(('replica', 'shard'))
- d_qkv_weight: float32 [768, 2304], P('shard')
- d_qv_bias: float32 [1536], P('shard')
- d_out_weight: float32 [768, 768], P('shard')
- d_out_bias: float32 [768], P('shard')
- d_first_gain: float32 [768], P('shard')
- d_first_shift: float32 [768], P('shard')
- d_up_weight: float32 [768, 3072], P('shard')
- d_up_bias: float32 [3072], P('shard')
- d_down_weight: float32 [3072, 768], P('shard')
- d_down_bias: float32 [768], P('shard')
- d_second_gain: float32 [768], P('shard')
- d_second_shift: float32 [768], P('shard')
The draws below stay inside these ranges and needn't reach their ends.
Inputs may be any that keep to these rules, and one draw needn't show every extreme that they name: Row b holds the lengths of the 4 sequences packed in order into token block b; a row sums to at most 128, and the slots after its sum are padding. Zero lengths occur. In every draw some row is one sequence of 128 tokens followed by empty ones.
All inputs are finite; a program needn't handle non-finite values.
Results may differ from the reference program's by a relative error of at most 0.018.
Values may be sent and summed in bfloat16 or wider, within the bound.
No kernel may reach another device: no remote copies, remote signals or barrier semaphores. Data moves between devices by JAX's collectives and lax.ppermute only.
A program may use at most 128 MiB of HBM per device.

```python
import math
import jax
import jax.numpy as jnp
from jax import lax

HEADS = 12
HEAD_DIM = 64
D = 768
FF = 3072
TOK_DEV = 128
SEQ_DEV = 4
TOKENS = 4096


def draw_lengths(key, part):
    key = jax.random.fold_in(key, 7)
    total_key, cut_key, full_key = jax.random.split(key, 3)
    blocks = TOKENS // TOK_DEV
    totals = jax.random.randint(total_key, (blocks, 1), TOK_DEV // 2, TOK_DEV + 1)
    cut_points = jnp.sort(jax.random.randint(cut_key, (blocks, SEQ_DEV - 1), 0, totals + 1), axis=1)
    bounds = jnp.concatenate([jnp.zeros((blocks, 1), jnp.int32), cut_points.astype(jnp.int32), totals.astype(jnp.int32)], axis=1)
    drawn = bounds[:, 1:] - bounds[:, :-1]
    chosen = jax.random.randint(full_key, (), 0, blocks)
    single = (jnp.arange(SEQ_DEV) == 0).astype(jnp.int32) * TOK_DEV
    return jnp.where((jnp.arange(blocks) == chosen)[:, None], single[None, :], drawn).astype(jnp.int32)


def strengthened(entries, stream_key, source, target, shards_of, factor):
    def block_of(axis_at):
        return (jnp.arange(entries.shape[axis_at]) // (entries.shape[axis_at] // shards_of)).reshape((-1,) + (1,) * (entries.ndim - 1 - axis_at))

    near = jax.random.permutation(stream_key, shards_of)[block_of(target)]
    far = (block_of(target) + shards_of // 2) % shards_of
    return jnp.where((block_of(source) == near) | (block_of(source) == far), factor * entries, entries)


def levels(own_key, extent, shards, smallest, top_value):
    def one(dim, shards_of):
        heights = jax.random.uniform(jax.random.fold_in(jax.random.fold_in(own_key, 6), dim), (shards_of,), jnp.float32, smallest / len(shards), top_value / len(shards))
        return jnp.repeat(jnp.exp(heights), extent[dim] // shards_of).reshape((-1,) + (1,) * (len(extent) - dim - 1))

    gain = one(*shards[0])
    for cut in shards[1:]:
        gain = gain * one(*cut)
    return gain


def normal_values(key, dims, scale, most, pieces=(), held_as=jnp.bfloat16):
    loudness = levels(key, dims, pieces, -0.22, 0.18) if pieces else 1.0
    entries = jax.random.normal(key, dims, jnp.float32) * scale * loudness
    return jnp.minimum(jnp.maximum(entries, -most), most).astype(held_as)


def bell_draw_with(own_key, extent, deviation, limit, cuts, heavy, kind=jnp.bfloat16):
    values = deviation * jax.random.normal(own_key, extent, jnp.float32)
    if cuts:
        values = values * levels(own_key, extent, cuts, -0.22, 0.18)
    return jnp.clip(strengthened(values, jax.random.fold_in(own_key, 3), *heavy), -limit, limit).astype(kind)


def setup_inputs(seed: int = 0) -> dict:
    seeds = jax.random.split(jax.random.key(seed), 16)
    tokens = normal_values(seeds[0], (TOKENS, D), 1.0, 6.0, ((0, 32),))
    lengths = draw_lengths(jax.random.fold_in(seeds[15], 71), 0)
    qkv_weight = normal_values(seeds[2], (D, 3 * D), D ** -0.5, 0.21875, ((0, 8),))
    qv_bias = normal_values(seeds[3], (2 * D,), 0.5, 3.0, ((0, 8),))
    out_weight = normal_values(seeds[4], (D, D), (D // 16) ** -0.5, 0.875, ((0, 8),))
    out_bias = normal_values(seeds[5], (D,), 0.3, 2.0, ((0, 8),))
    first_gain = jnp.clip(1.0 + 0.1 * jax.random.normal(seeds[6], (D,), jnp.float32), 0.5, 1.5).astype(jnp.bfloat16)
    first_shift = normal_values(seeds[7], (D,), 0.3, 2.0, ((0, 8),))
    up_weight = normal_values(seeds[8], (D, FF), D ** -0.5, 0.21875, ((0, 8),))
    up_bias = normal_values(seeds[9], (FF,), 0.5, 3.0, ((0, 8),))
    down_weight = normal_values(seeds[10], (FF, D), FF ** -0.5, 0.109375, ((0, 8),))
    down_bias = normal_values(seeds[11], (D,), 0.3, 2.0, ((0, 8),))
    second_gain = jnp.clip(1.0 + 0.1 * jax.random.normal(seeds[12], (D,), jnp.float32), 0.5, 1.5).astype(jnp.bfloat16)
    second_shift = normal_values(seeds[13], (D,), 0.3, 2.0, ((0, 8),))
    cotangent = bell_draw_with(seeds[14], (TOKENS, D), 1.0, 6.0, ((0, 32),), (0, 1, 32, 2.75))
    return {"tokens": tokens, "lengths": lengths, "qkv_weight": qkv_weight, "qv_bias": qv_bias, "out_weight": out_weight, "out_bias": out_bias, "first_gain": first_gain, "first_shift": first_shift, "up_weight": up_weight, "up_bias": up_bias, "down_weight": down_weight, "down_bias": down_bias, "second_gain": second_gain, "second_shift": second_shift, "cotangent": cotangent}


EPSILON = 1e-05
NEG_FILL = -1e+30
HIGH = lax.Precision.HIGHEST

@jax.custom_vjp
def low(v):
    return lax.optimization_barrier(v.astype(jnp.bfloat16)).astype(jnp.float32)

@jax.custom_vjp
def low_back(v):
    return v

def low_keep(v):
    return (low(v), None)

def low_pass(kept, grad):
    return (grad,)

def back_keep(v):
    return (v, None)

def back_low(kept, grad):
    return (low(grad),)
low.defvjp(low_keep, low_pass)
low_back.defvjp(back_keep, back_low)

def layout(length_rows):
    bounds = jnp.cumsum(length_rows, axis=-1).astype(jnp.int32)
    places = jnp.arange(TOK_DEV, dtype=jnp.int32)
    segment = lax.optimization_barrier(jnp.sum((places[:, None] >= bounds[..., None, :]).astype(jnp.int32), axis=-1)).astype(jnp.int32)
    usable = places < bounds[..., -1:]
    segment_id = jnp.where(usable, segment, SEQ_DEV + places)
    return (segment_id, usable)

def normalize(residual, norm_gain, norm_shift):
    center = residual - lax.optimization_barrier(jnp.mean(residual, axis=-1, keepdims=True))
    return center * lax.rsqrt(lax.optimization_barrier(jnp.mean(center * center, axis=-1, keepdims=True)) + EPSILON) * norm_gain + norm_shift

def project(left_side, right_side):
    return jnp.einsum('gnk,km->gnm', left_side, right_side, precision=HIGH)

def split_heads(tensor):
    return tensor.reshape(tensor.shape[:-1] + (HEADS, HEAD_DIM))

def layer(params, inputs, segment_id, usable):
    qkv_weight, qv_bias, out_weight, out_bias, first_gain, first_shift, up_weight, up_bias, down_weight, down_bias, second_gain, second_shift = params
    model_width = HEADS * HEAD_DIM
    projected = project(inputs, qkv_weight)
    queries = low_back(low(projected[..., :model_width] + qv_bias[:model_width]))
    key_rows = low_back(low(projected[..., model_width:2 * model_width]))
    values = low_back(low(projected[..., 2 * model_width:] + qv_bias[model_width:]))
    scores = low_back(jnp.einsum('gqhd,gkhd->ghqk', split_heads(queries), split_heads(key_rows), precision=HIGH) * HEAD_DIM ** (-0.5))
    same_segment = (segment_id[:, :, None] == segment_id[:, None, :])[:, None]
    masked = jnp.where(same_segment, scores, NEG_FILL)
    highest = lax.optimization_barrier(jnp.max(masked, axis=-1, keepdims=True))
    weights = jnp.exp(masked - highest)
    attn_probs = low(weights / lax.optimization_barrier(jnp.sum(weights, axis=-1, keepdims=True)))
    context = jnp.einsum('ghqk,gkhd->gqhd', attn_probs, split_heads(values), precision=HIGH).reshape(inputs.shape)
    context = low_back(low(context))
    attn_out = low_back(project(context, out_weight) + out_bias)
    hidden = normalize(inputs + attn_out, first_gain, first_shift)
    pre_act = low_back(project(low(hidden), up_weight) + up_bias)
    activated = low(jax.nn.gelu(pre_act, approximate=False))
    branch = low_back(project(activated, down_weight) + down_bias)
    result = normalize(hidden + branch, second_gain, second_shift)
    return result * usable[..., None].astype(result.dtype)

def reference(tokens, lengths, qkv_weight, qv_bias, out_weight, out_bias, first_gain, first_shift, up_weight, up_bias, down_weight, down_bias, second_gain, second_shift, cotangent):
    params = (qkv_weight.astype(jnp.float32), qv_bias.astype(jnp.float32), out_weight.astype(jnp.float32), out_bias.astype(jnp.float32), first_gain.astype(jnp.float32), first_shift.astype(jnp.float32), up_weight.astype(jnp.float32), up_bias.astype(jnp.float32), down_weight.astype(jnp.float32), down_bias.astype(jnp.float32), second_gain.astype(jnp.float32), second_shift.astype(jnp.float32))
    blocks = TOKENS // TOK_DEV
    per_step = math.gcd(blocks, max(1, 2560 // TOK_DEV))
    step_count = blocks // per_step
    model_width = HEADS * HEAD_DIM
    inputs = tokens.astype(jnp.float32).reshape(step_count, per_step, TOK_DEV, model_width)
    grads_in = cotangent.astype(jnp.float32).reshape(step_count, per_step, TOK_DEV, model_width)
    length_rows = lengths.reshape(step_count, per_step, SEQ_DEV)

    def advance(totals, inputs_now):
        block_in, block_grad, block_lengths = inputs_now
        segment_id, usable = layout(block_lengths)
        result, pullback = jax.vjp(lambda weight_set, activity: layer(weight_set, activity, segment_id, usable), params, block_in)
        grad_params, grad_activity = pullback(block_grad)
        totals = jax.tree.map(lambda first_term, other_term: first_term + other_term, totals, grad_params)
        return (totals, (result.astype(jnp.bfloat16), grad_activity.astype(jnp.bfloat16)))
    initial = jax.tree.map(jnp.zeros_like, params)
    totals, (results, grad_inputs) = lax.scan(advance, initial, (inputs, grads_in, length_rows))
    totals = tuple((entry.astype(jnp.float32) for entry in totals))
    return (results.reshape(TOKENS, model_width), grad_inputs.reshape(TOKENS, model_width), totals[0], totals[1], totals[2], totals[3], totals[4], totals[5], totals[6], totals[7], totals[8], totals[9], totals[10], totals[11])
```

```python
from functools import partial

import jax
import jax.numpy as jnp
from jax import lax
from jax.experimental import pallas as pl
from jax.experimental.pallas import tpu as pltpu
from jax.sharding import PartitionSpec as P

HEADS = 12


EPSILON = 1e-05
NEG_FILL = -1e30


def layout(length_row, row_count):
    bounds = jnp.cumsum(length_row)
    places = jnp.arange(row_count, dtype=jnp.int32)
    segment = jnp.sum((places[:, None] >= bounds[None, :]).astype(jnp.int32), axis=1)
    usable = places < bounds[-1]
    segment_id = jnp.where(usable, segment, length_row.shape[0] + places)
    return (segment_id, usable)


def matmul(left_side, right_side):
    return jnp.dot(left_side, right_side, preferred_element_type=jnp.float32)


def matmul_tn(left_side, right_side):
    return lax.dot_general(
        left_side, right_side, (((0,), (0,)), ((), ())), preferred_element_type=jnp.float32
    )


def matmul_nt(left_side, right_side):
    return lax.dot_general(
        left_side, right_side, (((1,), (1,)), ((), ())), preferred_element_type=jnp.float32
    )


def normalize(residual, norm_gain, norm_shift):
    center = residual - jnp.mean(residual, axis=1, keepdims=True)
    inverse = lax.rsqrt(jnp.mean(center * center, axis=1, keepdims=True) + EPSILON)
    normed = center * inverse
    return (normed * norm_gain + norm_shift, normed, inverse)


def normalize_back(grad_out, normed, inverse, norm_gain):
    scaled = grad_out * norm_gain
    grad_in = inverse * (
        scaled
        - jnp.mean(scaled, axis=1, keepdims=True)
        - normed * jnp.mean(scaled * normed, axis=1, keepdims=True)
    )
    return (grad_in, jnp.sum(grad_out * normed, axis=0), jnp.sum(grad_out, axis=0))


def split_heads(tensor):
    return tensor.reshape((tensor.shape[0], HEADS, tensor.shape[1] // HEADS))


def masked_scores(queries, key_rows, same_segment):
    scale_factor = (queries.shape[1] // HEADS) ** (-0.5)
    scores = (
        jnp.einsum(
            "qhd,khd->hqk",
            split_heads(queries),
            split_heads(key_rows),
            preferred_element_type=jnp.float32,
        )
        * scale_factor
    )
    return jnp.where(same_segment[None], scores, NEG_FILL)


def attend(queries, key_rows, values, same_segment):
    masked = masked_scores(queries, key_rows, same_segment)
    highest = jnp.max(masked, axis=2, keepdims=True)
    weights = jnp.exp(masked - highest)
    total = jnp.sum(weights, axis=2, keepdims=True)
    log_total = highest + jnp.log(total)
    attn_probs = (weights / total).astype(jnp.bfloat16)
    context = jnp.einsum(
        "hqk,khd->qhd", attn_probs, split_heads(values), preferred_element_type=jnp.float32
    )
    return (context.reshape(queries.shape).astype(jnp.bfloat16), log_total)


def attend_back(grad_context, queries, key_rows, values, same_segment, log_total):
    scale_factor = (queries.shape[1] // HEADS) ** (-0.5)
    masked = masked_scores(queries, key_rows, same_segment)
    attn_probs = jnp.exp(masked - log_total)
    probs_low = attn_probs.astype(jnp.bfloat16)
    grad_heads = split_heads(grad_context)
    grad_probs = jnp.einsum(
        "qhd,khd->hqk", grad_heads, split_heads(values), preferred_element_type=jnp.float32
    )
    grad_values = jnp.einsum(
        "hqk,qhd->khd", probs_low, grad_heads, preferred_element_type=jnp.float32
    )
    inner = jnp.sum(attn_probs * grad_probs, axis=2, keepdims=True)
    grad_scores = (attn_probs * (grad_probs - inner)).astype(jnp.bfloat16)
    grad_queries = (
        jnp.einsum(
            "hqk,khd->qhd", grad_scores, split_heads(key_rows), preferred_element_type=jnp.float32
        )
        * scale_factor
    )
    grad_keys = (
        jnp.einsum(
            "hqk,qhd->khd", grad_scores, split_heads(queries), preferred_element_type=jnp.float32
        )
        * scale_factor
    )
    shape_flat = queries.shape
    return (
        grad_queries.reshape(shape_flat).astype(jnp.bfloat16),
        grad_keys.reshape(shape_flat).astype(jnp.bfloat16),
        grad_values.reshape(shape_flat).astype(jnp.bfloat16),
    )


AXES = ("replica", "shard")
REPLICAS = 4
SHARDS = 8


def swap_pairs(dx, dcore, dz, dy):
    pairs = []
    for replica in range(REPLICAS):
        for shard in range(SHARDS):
            to_replica = replica ^ (dx * 2 + dcore)
            to_shard = shard ^ (dz * 2 + dy)
            pairs.append((replica * SHARDS + shard, to_replica * SHARDS + to_shard))
    return pairs


def swap_x(value):
    return lax.ppermute(value, AXES, swap_pairs(1, 0, 0, 0))


def swap_core(value):
    return lax.ppermute(value, AXES, swap_pairs(0, 1, 0, 0))


def swap_y(value):
    return lax.ppermute(value, AXES, swap_pairs(0, 0, 0, 1))


def swap_z(value, distance):
    return lax.ppermute(value, AXES, swap_pairs(0, 0, distance, 0))


def after(value, *others):
    return lax.optimization_barrier((value,) + others)[0]


def place_kernel(block_at, half, replica_shard, *refs):
    parts, whole, semaphores = refs[:-2], refs[-2], refs[-1]
    replica, shard = replica_shard[0], replica_shard[1]
    copies = []
    for core in range(2):
        for which in range(2):
            part = parts[core * 2 + which]
            for first in range(2):
                for second in range(2):
                    for z in range(4):
                        x, y = (first, second) if which == 0 else (second, first)
                        to_replica = replica ^ (x * 2 + core)
                        to_shard = shard ^ (z * 2 + y)
                        copy = pltpu.make_async_copy(
                            part.at[first, second, z],
                            block_at(whole, to_replica, to_shard, which * half, half),
                            semaphores.at[len(copies)],
                        )
                        copy.start()
                        copies.append(copy)
    for copy in copies:
        copy.wait()


def split_kernel(block_at, half, replica_shard, whole, *refs):
    parts, semaphores = refs[:-1], refs[-1]
    replica, shard = replica_shard[0], replica_shard[1]
    copies = []
    for core in (1, 0):
        for which in range(2):
            part = parts[core * 2 + which]
            for first in range(2):
                for second in range(2):
                    for z in range(4):
                        x, y = (first, second) if which == 0 else (second, first)
                        to_replica = replica ^ (x * 2 + core)
                        to_shard = shard ^ (z * 2 + y)
                        copy = pltpu.make_async_copy(
                            block_at(whole, to_replica, to_shard, which * half, half),
                            part.at[first, second, z],
                            semaphores.at[len(copies)],
                        )
                        copy.start()
                        copies.append(copy)
    for copy in copies:
        copy.wait()


def block_columns(whole, replica, shard, start, half):
    width = whole.shape[1] // REPLICAS
    height = whole.shape[0] // SHARDS
    return whole.at[
        pl.ds(pl.multiple_of(shard * height + start, 16), half),
        pl.ds(pl.multiple_of(replica * width, 128), width),
    ]


def block_rows(whole, replica, shard, start, half):
    height = whole.shape[0] // (SHARDS * REPLICAS)
    return whole.at[
        pl.ds(pl.multiple_of((shard * REPLICAS + replica) * height + start, 16), half), :
    ]


def place(parts, shape, block_at, position):
    half = parts[0].shape[3]
    return pl.pallas_call(
        partial(place_kernel, block_at, half),
        out_shape=jax.ShapeDtypeStruct(shape, parts[0].dtype),
        in_specs=[pl.BlockSpec(memory_space=pltpu.SMEM)]
        + [pl.BlockSpec(memory_space=pl.ANY)] * 4,
        out_specs=pl.BlockSpec(memory_space=pltpu.VMEM),
        compiler_params=pltpu.CompilerParams(vmem_limit_bytes=16 * 2**20),
        scratch_shapes=[pltpu.SemaphoreType.DMA((64,))],
        name="place",
    )(position, *parts)


def split(whole, half, width, block_at, position):
    shape = jax.ShapeDtypeStruct((2, 2, 4, half, width), whole.dtype)
    return pl.pallas_call(
        partial(split_kernel, block_at, half),
        out_shape=[shape] * 4,
        in_specs=[
            pl.BlockSpec(memory_space=pltpu.SMEM),
            pl.BlockSpec(memory_space=pltpu.VMEM),
        ],
        out_specs=[pl.BlockSpec(memory_space=pl.ANY)] * 4,
        compiler_params=pltpu.CompilerParams(vmem_limit_bytes=16 * 2**20),
        scratch_shapes=[pltpu.SemaphoreType.DMA((64,))],
        name="split",
    )(position, whole)


def gather_z(piece):
    received = [swap_z(piece, distance) for distance in (1, 2, 3)]
    half = piece.shape[0] // 2
    return [
        jnp.stack([entry[which * half : (which + 1) * half] for entry in [piece] + received])
        for which in range(2)
    ]


def gather_xy(halves):
    y_first, x_first = halves
    y_pair = jnp.stack([y_first, swap_y(y_first)])
    x_pair = jnp.stack([x_first, swap_x(x_first)])
    y_all = jnp.stack([y_pair, swap_x(y_pair)])
    x_all = jnp.stack([x_pair, swap_y(x_pair)])
    return (y_all, x_all)


def gather_core(pair):
    y_all, x_all = pair
    return (y_all, x_all, swap_core(y_all), swap_core(x_all))


def plus(left_side, right_side):
    return (left_side.astype(jnp.float32) + right_side.astype(jnp.float32)).astype(jnp.bfloat16)


def reduce_chunk(parts):
    mine_x, mine_y, other_x, other_y = parts
    sum_x = plus(mine_x, swap_core(other_x))
    sum_y = plus(mine_y, swap_core(other_y))
    sum_x = plus(sum_x[0], swap_x(sum_x[1]))
    sum_y = plus(sum_y[0], swap_y(sum_y[1]))
    sum_x = plus(sum_x[0], swap_y(sum_x[1]))
    sum_y = plus(sum_y[0], swap_x(sum_y[1]))
    both = jnp.concatenate([sum_x, sum_y], axis=1)
    total = both[0].astype(jnp.float32)
    for distance in (1, 2, 3):
        total = total + swap_z(both[distance], distance).astype(jnp.float32)
    return total.astype(jnp.bfloat16)


def spread(quarter, x, core):
    other = swap_x(quarter)
    pair = jnp.stack([jnp.where(x == 0, quarter, other), jnp.where(x == 0, other, quarter)])
    far = swap_core(pair)
    return jnp.stack(
        [jnp.where(core == 0, pair, far), jnp.where(core == 0, far, pair)], axis=1
    ).reshape((REPLICAS,) + quarter.shape)


def small_gather(vector, z, y):
    block = vector[None]
    other = swap_y(block)
    block = jnp.concatenate([jnp.where(y == 0, block, other), jnp.where(y == 0, other, block)])
    for distance in (1, 2):
        other = swap_z(block, distance)
        low_side = (z & distance) == 0
        block = jnp.concatenate(
            [jnp.where(low_side, block, other), jnp.where(low_side, other, block)]
        )
    return block


def small_sum(vector):
    vector = vector + swap_core(vector)
    vector = vector + swap_x(vector)
    vector = vector + swap_y(vector)
    vector = vector + swap_z(vector, 1)
    return vector + swap_z(vector, 2)


def on_device(
    mesh_shape,
    tokens,
    lengths,
    qkv_weight,
    qv_bias,
    out_weight,
    out_bias,
    first_gain,
    first_shift,
    up_weight,
    up_bias,
    down_weight,
    down_bias,
    second_gain,
    second_shift,
    cotangent,
):
    model_width = tokens.shape[1]
    replica = lax.axis_index("replica").astype(jnp.int32)
    shard = lax.axis_index("shard").astype(jnp.int32)
    x, core, z, y = replica // 2, replica % 2, shard // 2, shard % 2
    direct = mesh_shape["replica"] == REPLICAS and mesh_shape["shard"] == SHARDS
    position = jnp.stack([replica, shard])
    segment_id, usable = layout(lengths[0], tokens.shape[0])
    same_segment = segment_id[:, None] == segment_id[None, :]
    keep_rows = usable.astype(jnp.float32)[:, None]
    small = (qv_bias, out_bias, first_gain, first_shift, up_bias, down_bias, second_gain, second_shift)
    sizes = [entry.shape[0] for entry in small]
    if direct:
        packed = small_gather(jnp.concatenate(small), z, y)
        quarter_attn = lax.switch(
            replica,
            [lambda at=at: qkv_weight[:, at * 768 : (at + 1) * 768] for at in range(3)]
            + [lambda: out_weight],
        )
        quarter_up = lax.dynamic_slice_in_dim(up_weight, replica * 768, 768, axis=1)
        quarter_down = lax.dynamic_slice_in_dim(down_weight, replica * 96, 96, axis=0)
        z_attn = gather_z(quarter_attn)
        quarter_up = after(quarter_up, *z_attn)
        xy_attn = gather_xy(z_attn)
        z_up = gather_z(quarter_up)
        quarter_down = after(quarter_down, *z_up)
        z_up = [after(entry, *xy_attn) for entry in z_up]
        core_attn = gather_core(xy_attn)
        z_down = gather_z(quarter_down)
        xy_up = gather_xy(z_up)
        z_down = [after(entry, *xy_up) for entry in z_down]
        core_up = gather_core(xy_up)
        xy_down = gather_xy(z_down)
        core_down = gather_core(xy_down)
        w_attn = place(core_attn, (768, 3072), block_columns, position)
        w_qkv, w_out = w_attn[:, : 3 * model_width], w_attn[:, 3 * model_width :]
        w_up = place(core_up, (768, 3072), block_columns, position)
        w_down = place(core_down, (3072, 768), block_rows, position)
    else:
        packed = lax.all_gather(jnp.concatenate(small), "shard", axis=0)
        w_qkv, w_out, w_up, w_down = (
            lax.all_gather(entry, "shard", axis=0, tiled=True)
            for entry in (qkv_weight, out_weight, up_weight, down_weight)
        )
    ends = [sum(sizes[:count]) for count in range(len(sizes) + 1)]
    b_qv, b_out, gain_one, shift_one, b_up, b_down, gain_two, shift_two = (
        packed[:, ends[at] : ends[at + 1]].reshape(-1) for at in range(len(sizes))
    )
    projected = matmul(tokens, w_qkv)
    bias_full = b_qv.astype(jnp.float32)
    queries = (projected[:, :model_width] + bias_full[:model_width]).astype(jnp.bfloat16)
    key_rows = projected[:, model_width : 2 * model_width].astype(jnp.bfloat16)
    values = (projected[:, 2 * model_width :] + bias_full[model_width:]).astype(jnp.bfloat16)
    context, log_total = attend(queries, key_rows, values, same_segment)
    attn_out = matmul(context, w_out) + b_out.astype(jnp.float32)
    gain_first = gain_one.astype(jnp.float32)
    hidden, normed_one, inverse_one = normalize(
        tokens.astype(jnp.float32) + attn_out, gain_first, shift_one.astype(jnp.float32)
    )
    hidden_low = hidden.astype(jnp.bfloat16)
    pre_act = matmul(hidden_low, w_up) + b_up.astype(jnp.float32)
    activated = jax.nn.gelu(pre_act, approximate=False).astype(jnp.bfloat16)
    branch = matmul(activated, w_down) + b_down.astype(jnp.float32)
    gain_second = gain_two.astype(jnp.float32)
    output_full, normed_two, inverse_two = normalize(
        hidden + branch, gain_second, shift_two.astype(jnp.float32)
    )
    layer_out = (output_full * keep_rows).astype(jnp.bfloat16)
    grad_out = cotangent.astype(jnp.float32) * keep_rows
    grad_second, grad_gain_two, grad_shift_two = normalize_back(
        grad_out, normed_two, inverse_two, gain_second
    )
    grad_branch = grad_second.astype(jnp.bfloat16)
    grad_w_down = matmul_tn(activated, grad_branch).astype(jnp.bfloat16)
    if direct:
        parts_down = split(grad_w_down, 48, 768, block_rows, position)
        reduced_down = reduce_chunk(parts_down)
    grad_b_down = jnp.sum(grad_branch.astype(jnp.float32), axis=0)
    grad_act = matmul_nt(grad_branch, w_down)
    gelu_value, gelu_pull = jax.vjp(partial(jax.nn.gelu, approximate=False), pre_act)
    grad_pre = gelu_pull(grad_act)[0].astype(jnp.bfloat16)
    grad_w_up = matmul_tn(hidden_low, grad_pre).astype(jnp.bfloat16)
    if direct:
        parts_up = split(grad_w_up, 48, 768, block_columns, position)
        reduced_up = reduce_chunk(parts_up)
    grad_b_up = jnp.sum(grad_pre.astype(jnp.float32), axis=0)
    grad_hidden = grad_second + matmul_nt(grad_pre, w_up)
    grad_first, grad_gain_one, grad_shift_one = normalize_back(
        grad_hidden, normed_one, inverse_one, gain_first
    )
    grad_attn = grad_first.astype(jnp.bfloat16)
    grad_w_out = matmul_tn(context, grad_attn).astype(jnp.bfloat16)
    grad_b_out = jnp.sum(grad_attn.astype(jnp.float32), axis=0)
    grad_context = matmul_nt(grad_attn, w_out).astype(jnp.bfloat16)
    grad_queries, grad_keys, grad_values = attend_back(
        grad_context, queries, key_rows, values, same_segment, log_total
    )
    grad_proj = jnp.concatenate([grad_queries, grad_keys, grad_values], axis=1)
    grad_w_qkv = matmul_tn(tokens, grad_proj).astype(jnp.bfloat16)
    grad_b_qv = jnp.concatenate(
        [
            jnp.sum(grad_queries.astype(jnp.float32), axis=0),
            jnp.sum(grad_values.astype(jnp.float32), axis=0),
        ]
    )
    grad_tokens = (grad_first + matmul_nt(grad_proj, w_qkv)).astype(jnp.bfloat16)
    small_grads = (
        grad_b_qv,
        grad_b_out,
        grad_gain_one,
        grad_shift_one,
        grad_b_up,
        grad_b_down,
        grad_gain_two,
        grad_shift_two,
    )
    shards = mesh_shape["shard"]
    packed_grads = jnp.concatenate([entry.reshape(shards, -1) for entry in small_grads], axis=1)
    if direct:
        parts_attn = split(
            jnp.concatenate([grad_w_qkv, grad_w_out], axis=1), 48, 768, block_columns, position
        )
        reduced_attn = reduce_chunk(parts_attn)
        small_total = lax.dynamic_index_in_dim(small_sum(packed_grads), shard, 0, False)
        d_down = spread(reduced_down, x, core).reshape(-1, 768).astype(jnp.float32)
        up_quarters = spread(reduced_up, x, core).astype(jnp.float32)
        d_up = jnp.concatenate([up_quarters[at] for at in range(REPLICAS)], axis=1)
        attn_quarters = spread(reduced_attn, x, core).astype(jnp.float32)
        d_qkv = jnp.concatenate([attn_quarters[at] for at in range(3)], axis=1)
        d_out = attn_quarters[3]
    else:
        d_down, d_up, d_qkv, d_out = (
            lax.psum(
                lax.psum_scatter(entry, "shard", scatter_dimension=0, tiled=True), "replica"
            ).astype(jnp.float32)
            for entry in (grad_w_down, grad_w_up, grad_w_qkv, grad_w_out)
        )
        small_total = lax.psum(
            lax.psum_scatter(packed_grads, "shard", scatter_dimension=0, tiled=True), "replica"
        ).reshape(-1)
    small_outs = [small_total[ends[at] : ends[at + 1]] for at in range(len(sizes))]
    return (
        layer_out,
        grad_tokens,
        d_qkv,
        small_outs[0],
        d_out,
        small_outs[1],
        small_outs[2],
        small_outs[3],
        d_up,
        small_outs[4],
        d_down,
        small_outs[5],
        small_outs[6],
        small_outs[7],
    )


def solution(mesh):
    placed = (
        P(("replica", "shard"), None),
        P(("replica", "shard"), None),
        P("shard", None),
        P("shard"),
        P("shard", None),
        P("shard"),
        P("shard"),
        P("shard"),
        P("shard", None),
        P("shard"),
        P("shard", None),
        P("shard"),
        P("shard"),
        P("shard"),
        P(("replica", "shard"), None),
    )
    return jax.shard_map(
        partial(on_device, dict(mesh.shape)),
        mesh=mesh,
        in_specs=placed,
        out_specs=(
            P(("replica", "shard"), None),
            P(("replica", "shard"), None),
            P("shard", None),
            P("shard"),
            P("shard", None),
            P("shard"),
            P("shard"),
            P("shard"),
            P("shard", None),
            P("shard"),
            P("shard", None),
            P("shard"),
            P("shard"),
            P("shard"),
        ),
        check_vma=False,
    )
```

```python
from functools import partial

import jax
import jax.numpy as jnp
from jax import lax
from jax.experimental import pallas as pl
from jax.experimental.pallas import tpu as pltpu
from jax.sharding import PartitionSpec as P

HEADS = 12


EPSILON = 1e-05
NEG_FILL = -1e30


def layout(length_row, row_count):
    bounds = jnp.cumsum(length_row)
    places = jnp.arange(row_count, dtype=jnp.int32)
    segment = jnp.sum((places[:, None] >= bounds[None, :]).astype(jnp.int32), axis=1)
    usable = places < bounds[-1]
    segment_id = jnp.where(usable, segment, length_row.shape[0] + places)
    return (segment_id, usable)


def matmul(left_side, right_side):
    return jnp.dot(left_side, right_side, preferred_element_type=jnp.float32)


def matmul_tn(left_side, right_side):
    return lax.dot_general(
        left_side, right_side, (((0,), (0,)), ((), ())), preferred_element_type=jnp.float32
    )


def matmul_nt(left_side, right_side):
    return lax.dot_general(
        left_side, right_side, (((1,), (1,)), ((), ())), preferred_element_type=jnp.float32
    )


def normalize(residual, norm_gain, norm_shift):
    center = residual - jnp.mean(residual, axis=1, keepdims=True)
    inverse = lax.rsqrt(jnp.mean(center * center, axis=1, keepdims=True) + EPSILON)
    normed = center * inverse
    return (normed * norm_gain + norm_shift, normed, inverse)


def normalize_back(grad_out, normed, inverse, norm_gain):
    scaled = grad_out * norm_gain
    grad_in = inverse * (
        scaled
        - jnp.mean(scaled, axis=1, keepdims=True)
        - normed * jnp.mean(scaled * normed, axis=1, keepdims=True)
    )
    return (grad_in, jnp.sum(grad_out * normed, axis=0), jnp.sum(grad_out, axis=0))


def split_heads(tensor):
    return tensor.reshape((tensor.shape[0], HEADS, tensor.shape[1] // HEADS))


def masked_scores(queries, key_rows, same_segment):
    scale_factor = (queries.shape[1] // HEADS) ** (-0.5)
    scores = (
        jnp.einsum(
            "qhd,khd->hqk",
            split_heads(queries),
            split_heads(key_rows),
            preferred_element_type=jnp.float32,
        )
        * scale_factor
    )
    return jnp.where(same_segment[None], scores, NEG_FILL)


def attend(queries, key_rows, values, same_segment):
    masked = masked_scores(queries, key_rows, same_segment)
    highest = jnp.max(masked, axis=2, keepdims=True)
    weights = jnp.exp(masked - highest)
    total = jnp.sum(weights, axis=2, keepdims=True)
    log_total = highest + jnp.log(total)
    attn_probs = (weights / total).astype(jnp.bfloat16)
    context = jnp.einsum(
        "hqk,khd->qhd", attn_probs, split_heads(values), preferred_element_type=jnp.float32
    )
    return (context.reshape(queries.shape).astype(jnp.bfloat16), log_total)


def attend_back(grad_context, queries, key_rows, values, same_segment, log_total):
    scale_factor = (queries.shape[1] // HEADS) ** (-0.5)
    masked = masked_scores(queries, key_rows, same_segment)
    attn_probs = jnp.exp(masked - log_total)
    probs_low = attn_probs.astype(jnp.bfloat16)
    grad_heads = split_heads(grad_context)
    grad_probs = jnp.einsum(
        "qhd,khd->hqk", grad_heads, split_heads(values), preferred_element_type=jnp.float32
    )
    grad_values = jnp.einsum(
        "hqk,qhd->khd", probs_low, grad_heads, preferred_element_type=jnp.float32
    )
    inner = jnp.sum(attn_probs * grad_probs, axis=2, keepdims=True)
    grad_scores = (attn_probs * (grad_probs - inner)).astype(jnp.bfloat16)
    grad_queries = (
        jnp.einsum(
            "hqk,khd->qhd", grad_scores, split_heads(key_rows), preferred_element_type=jnp.float32
        )
        * scale_factor
    )
    grad_keys = (
        jnp.einsum(
            "hqk,qhd->khd", grad_scores, split_heads(queries), preferred_element_type=jnp.float32
        )
        * scale_factor
    )
    shape_flat = queries.shape
    return (
        grad_queries.reshape(shape_flat).astype(jnp.bfloat16),
        grad_keys.reshape(shape_flat).astype(jnp.bfloat16),
        grad_values.reshape(shape_flat).astype(jnp.bfloat16),
    )


AXES = ("replica", "shard")
REPLICAS = 4
SHARDS = 8


def swap_pairs(dx, dcore, dz, dy):
    pairs = []
    for replica in range(REPLICAS):
        for shard in range(SHARDS):
            to_replica = replica ^ (dx * 2 + dcore)
            to_shard = shard ^ (dz * 2 + dy)
            pairs.append((replica * SHARDS + shard, to_replica * SHARDS + to_shard))
    return pairs


def swap_x(value):
    return lax.ppermute(value, AXES, swap_pairs(1, 0, 0, 0))


def swap_core(value):
    return lax.ppermute(value, AXES, swap_pairs(0, 1, 0, 0))


def swap_y(value):
    return lax.ppermute(value, AXES, swap_pairs(0, 0, 0, 1))


def swap_z(value, distance):
    return lax.ppermute(value, AXES, swap_pairs(0, 0, distance, 0))


def after(value, *others):
    return lax.optimization_barrier((value,) + others)[0]


def share(block):
    across = swap_x(block)
    return [block, swap_core(block), across, swap_core(across)]


def collect(near, far):
    pair = plus(near, swap_core(far))
    return pair[0], swap_x(pair[1])


def swap_zs(piece):
    return [piece] + [swap_z(piece, distance) for distance in (1, 2, 3)]


def halves_of(pieces):
    half = pieces[0].shape[0] // 2
    return [jnp.stack([entry[at : at + half] for entry in pieces]) for at in (0, half)]


def cross_first(halves):
    return [swap_y(halves[0]), swap_x(halves[1])]


def near_of(halves, come):
    return [jnp.stack(pair) for pair in zip(halves, come)]


def cross_second(near):
    return [swap_x(near[0]), swap_y(near[1])]


def swap_cores(parts):
    return [swap_core(entry) for entry in parts]


def parts_of(near, far, core_near, core_far):
    return [entry for group in zip(near, far, core_near, core_far) for entry in group]


def route(leading, start, rows):
    return [(leading, fixed, core, start, rows) for core in range(2) for fixed in range(2)]


PLAN = route("y", 0, 48) + route("x", 48, 48)


def plus(left_side, right_side):
    return (left_side.astype(jnp.float32) + right_side.astype(jnp.float32)).astype(jnp.bfloat16)


def swap_parts(parts):
    return [swap_core(parts[at]) for at in (3, 7, 2, 6)]


def sum_parts(parts, come):
    far = [plus(parts[1], come[0]), plus(parts[5], come[1])]
    return far, [plus(parts[0], come[2]), plus(parts[4], come[3])]


def sum_plane(near, come):
    onward = [plus(mine[1], other[1]) for mine, other in zip(near, come)]
    return onward, [plus(mine[0], other[0]) for mine, other in zip(near, come)]


def sum_last(stay, come):
    return jnp.concatenate([plus(mine, other) for mine, other in zip(stay, come)], axis=1)


def send_zs(block):
    return [swap_z(block[distance], distance) for distance in (1, 2, 3)]


def sum_zs(block, come):
    total = block[0].astype(jnp.float32)
    for entry in come:
        total = total + entry.astype(jnp.float32)
    return total.astype(jnp.bfloat16)


def spread(quarter, x, core):
    other = swap_x(quarter)
    pair = jnp.stack([jnp.where(x == 0, quarter, other), jnp.where(x == 0, other, quarter)])
    far = swap_core(pair)
    return jnp.stack(
        [jnp.where(core == 0, pair, far), jnp.where(core == 0, far, pair)], axis=1
    ).reshape((REPLICAS,) + quarter.shape)


KERNEL_VMEM = 24 * 2**20
ROOT_HALF = 0.7071067811865476
ROOT_TWO_PI = 0.3989422804014327
VMEM = pl.BlockSpec(memory_space=pltpu.VMEM)
SMEM = pl.BlockSpec(memory_space=pltpu.SMEM)
ROWS_OF = (2, 1, 1, 1, 4, 1, 1, 1)


def kernel_call(kernel, name, out_shapes, inputs, scratch=(), scalars=1):
    return pl.pallas_call(
        kernel,
        out_shape=tuple(out_shapes),
        in_specs=[SMEM] * scalars + [VMEM] * (len(inputs) - scalars),
        out_specs=(VMEM,) * len(out_shapes),
        scratch_shapes=list(scratch),
        compiler_params=pltpu.CompilerParams(vmem_limit_bytes=KERNEL_VMEM),
        cost_estimate=pl.CostEstimate(flops=2**20, bytes_accessed=2**20, transcendentals=0),
        name=name,
    )(*inputs)


def places(replica, shard):
    for at, (leading, fixed, core, start, count) in enumerate(PLAN):
        for first in range(2):
            x, y = (first, fixed) if leading == "x" else (fixed, first)
            columns = pl.ds(pl.multiple_of((replica ^ (x * 2 + core)) * 768, 128), 768)
            for z in range(4):
                owner = shard ^ (z * 2 + y)
                rows = pl.ds(pl.multiple_of(owner * 96 + start, 16), count)
                yield at, first, z, rows, columns


def segments(lengths, dim, shape):
    at = lax.broadcasted_iota(jnp.int32, shape, dim)
    bound = jnp.int32(0)
    segment = jnp.zeros(shape, jnp.int32)
    for sequence in range(lengths.shape[1]):
        bound = bound + lengths[0, sequence]
        segment = segment + (at >= bound).astype(jnp.int32)
    return jnp.where(at < bound, segment, lengths.shape[1] + at), at < bound


def head_masks(width):
    lane = lax.broadcasted_iota(jnp.int32, (1, width), 1)
    low = lane < width // 2
    return low, [low.astype(jnp.bfloat16), 1.0 - low.astype(jnp.bfloat16)]


def attend_kernel(position, lengths, tokens, packed, *refs):
    parts, refs = refs[:8], refs[8:]
    whole, proj, weights, context, hidden, hidden_low, normed_one, inverse_one, table, keep = refs
    for at, first, z, rows, columns in places(position[0], position[1]):
        whole[rows, columns] = parts[at][first, z]
    pieces = packed[...].astype(jnp.float32)
    row, column = 0, 0
    for count in ROWS_OF:
        for at in range(count):
            if count == 2:
                owners = range(at * 4, at * 4 + 4)
                values = [pieces[owner : owner + 1, 0:192] for owner in owners]
            else:
                start = column + at * 96
                values = [pieces[owner : owner + 1, start : start + 96] for owner in range(SHARDS)]
            table[row : row + 1, :] = jnp.concatenate(values, axis=1)
            row += 1
        column += count * 96
    for step in range(3):
        columns = slice(step * 768, (step + 1) * 768)
        projected = matmul(tokens[...], whole[:, columns])
        if step == 0:
            projected = projected + table[0:1, :]
        if step == 2:
            projected = projected + table[1:2, :]
        proj[:, columns] = projected.astype(jnp.bfloat16)
    count = tokens.shape[0]
    across, usable = segments(lengths, 0, (count, 1))
    along, _ = segments(lengths, 1, (1, count))
    keep[...] = usable.astype(jnp.float32)
    same = across == along
    low, masks = head_masks(128)
    for pair in range(HEADS // 2):
        queries, key_rows, values = (
            proj[:, step * 768 + pair * 128 : step * 768 + (pair + 1) * 128] for step in range(3)
        )
        sums = []
        for which in range(2):
            scores = matmul_nt(queries * masks[which], key_rows) * 0.125
            masked = jnp.where(same, scores, NEG_FILL)
            entries = jnp.exp(masked - jnp.max(masked, axis=1, keepdims=True))
            share_of = entries / jnp.sum(entries, axis=1, keepdims=True)
            weights[pair * 2 + which] = share_of
            sums.append(matmul(share_of.astype(jnp.bfloat16), values))
        context[:, pair * 128 : (pair + 1) * 128] = jnp.where(low, sums[0], sums[1]).astype(
            jnp.bfloat16
        )
    attn_out = matmul(context[...], whole[:, 2304:]) + table[2:3, :]
    result, normed, inverse = normalize(
        tokens[...].astype(jnp.float32) + attn_out, table[3:4, :], table[4:5, :]
    )
    hidden[...] = result
    hidden_low[...] = result.astype(jnp.bfloat16)
    normed_one[...] = normed
    inverse_one[...] = inverse


def column_sum(values):
    return jnp.sum(values.astype(jnp.float32), axis=0, keepdims=True)


def attend_back_kernel(
    position,
    mine,
    come,
    grad_second,
    normed_one,
    inverse_one,
    table,
    context,
    proj,
    weights,
    whole,
    tokens,
    *refs,
):
    parts, refs = refs[:8], refs[8:]
    grad_first, grad_proj, small, total = refs
    grad_hidden = grad_second[...] + (mine[...].astype(jnp.float32) + come[...].astype(jnp.float32))
    grad_in, grad_gain, grad_shift = normalize_back(
        grad_hidden, normed_one[...], inverse_one[...], table[3:4, :]
    )
    grad_first[...] = grad_in
    grad_attn = grad_in.astype(jnp.bfloat16)
    small[2:3, :] = column_sum(grad_attn)
    small[3:4, :] = grad_gain[None, :]
    small[4:5, :] = grad_shift[None, :]
    total[:, 2304:] = matmul_tn(context[...], grad_attn).astype(jnp.bfloat16)
    grad_context = matmul_nt(grad_attn, whole[:, 2304:]).astype(jnp.bfloat16)
    low, masks = head_masks(128)
    for pair in range(HEADS // 2):
        queries, key_rows, values = (
            proj[:, step * 768 + pair * 128 : step * 768 + (pair + 1) * 128] for step in range(3)
        )
        grad_pair = grad_context[:, pair * 128 : (pair + 1) * 128]
        sums = []
        for which in range(2):
            share_of = weights[pair * 2 + which]
            grad_probs = matmul_nt(grad_pair * masks[which], values)
            inner = jnp.sum(share_of * grad_probs, axis=1, keepdims=True)
            grad_scores = (share_of * (grad_probs - inner)).astype(jnp.bfloat16)
            sums.append(
                (
                    matmul(grad_scores, key_rows) * 0.125,
                    matmul_tn(grad_scores, queries) * 0.125,
                    matmul_tn(share_of.astype(jnp.bfloat16), grad_pair),
                )
            )
        for step in range(3):
            grad_proj[:, step * 768 + pair * 128 : step * 768 + (pair + 1) * 128] = jnp.where(
                low, sums[0][step], sums[1][step]
            ).astype(jnp.bfloat16)
    for step in range(3):
        columns = slice(step * 768, (step + 1) * 768)
        total[:, columns] = matmul_tn(tokens[...], grad_proj[:, columns]).astype(jnp.bfloat16)
    small[0:1, :] = column_sum(grad_proj[:, :768])
    small[1:2, :] = column_sum(grad_proj[:, 1536:])
    for at, first, z, rows, columns in places(position[0], position[1]):
        parts[at][first, z] = total[rows, columns]


def tokens_kernel(position, grad_first, grad_proj, whole, grad_tokens):
    grad_tokens[...] = (grad_first[...] + matmul_nt(grad_proj[...], whole[:, :2304])).astype(
        jnp.bfloat16
    )


def fill(whole, near, far, shard):
    for y, part in enumerate((near, far)):
        for z in range(4):
            owner = shard ^ (z * 2 + y)
            whole[pl.ds(pl.multiple_of(owner * 96, 16), 96), :] = part[z]


def drain(near, far, whole, shard):
    for y, part in enumerate((near, far)):
        for z in range(4):
            owner = shard ^ (z * 2 + y)
            part[z] = whole[pl.ds(pl.multiple_of(owner * 96, 16), 96), :]


def feed_kernel(
    position, own, from_core, from_x, from_both, table, up_near, up_far, down_near, down_far, *outs
):
    w_up, w_down, activated, slope, near, far = outs
    fill(w_up, up_near, up_far, position[1])
    fill(w_down, down_near, down_far, position[1])
    bias = table[pl.ds(5 + position[0], 1), :]
    spots = ((near, 0), (far, 0), (near, 1), (far, 1))
    for step, block in enumerate((own, from_core, from_x, from_both)):
        rows = slice(step * 128, (step + 1) * 128)
        pre_act = matmul(block[...], w_up[...]) + bias
        below = 0.5 * (1.0 + lax.erf(pre_act * ROOT_HALF))
        active = (pre_act * below).astype(jnp.bfloat16)
        activated[rows, :] = active
        slope[rows, :] = below + pre_act * (ROOT_TWO_PI * jnp.exp(-0.5 * pre_act * pre_act))
        out, at = spots[step]
        out[at] = matmul(active, w_down[...]).astype(jnp.bfloat16)


def close_kernel(position, mine, come, hidden, table, keep, cotangent, *outs):
    layer_out, grad_second, grad_branch, small = outs
    gain = table[10:11, :]
    branch = mine[...].astype(jnp.float32) + come[...].astype(jnp.float32) + table[9:10, :]
    output_full, normed, inverse = normalize(hidden[...] + branch, gain, table[11:12, :])
    layer_out[...] = (output_full * keep[...]).astype(jnp.bfloat16)
    grad_out = cotangent[...].astype(jnp.float32) * keep[...]
    grad_in, grad_gain, grad_shift = normalize_back(grad_out, normed, inverse, gain)
    low_grad = grad_in.astype(jnp.bfloat16)
    grad_second[...] = grad_in
    grad_branch[...] = low_grad
    small[0:1, :] = jnp.sum(low_grad.astype(jnp.float32), axis=0, keepdims=True)
    small[1:2, :] = grad_gain[None, :]
    small[2:3, :] = grad_shift[None, :]


def back_kernel(position, own, from_core, from_x, from_both, slope, w_up, w_down, *outs):
    grad_pre, near, far, small = outs
    spots = ((near, 0), (far, 0), (near, 1), (far, 1))
    total = jnp.zeros((1, slope.shape[1]), jnp.float32)
    for step, block in enumerate((own, from_core, from_x, from_both)):
        rows = slice(step * 128, (step + 1) * 128)
        grad = matmul_nt(block[...], w_down[...]) * slope[rows, :]
        low_grad = grad.astype(jnp.bfloat16)
        grad_pre[rows, :] = low_grad
        total = total + jnp.sum(low_grad.astype(jnp.float32), axis=0, keepdims=True)
        out, at = spots[step]
        out[at] = matmul_nt(low_grad, w_up[...]).astype(jnp.bfloat16)
    small[...] = total


def weight_kernel(count, position, *refs):
    blocks, right, (near, far, total) = refs[:count], refs[count:-3], refs[-3:]
    if count == 1:
        total[...] = matmul_tn(blocks[0][...], joined(right)).astype(jnp.bfloat16)
    else:
        total[...] = matmul_tn(joined(blocks), right[0][...]).astype(jnp.bfloat16)
    drain(near, far, total, position[1])


def joined(refs):
    return jnp.concatenate([entry[...] for entry in refs], axis=0)


def small_gather(vector, z, y):
    block = vector[None]
    other = swap_y(block)
    block = jnp.concatenate([jnp.where(y == 0, block, other), jnp.where(y == 0, other, block)])
    for distance in (1, 2):
        other = swap_z(block, distance)
        low_side = (z & distance) == 0
        block = jnp.concatenate(
            [jnp.where(low_side, block, other), jnp.where(low_side, other, block)]
        )
    return block


def small_sum(vector):
    vector = vector + swap_core(vector)
    vector = vector + swap_x(vector)
    vector = vector + swap_y(vector)
    vector = vector + swap_z(vector, 1)
    return vector + swap_z(vector, 2)


def on_device_general(
    tokens,
    lengths,
    qkv_weight,
    qv_bias,
    out_weight,
    out_bias,
    first_gain,
    first_shift,
    up_weight,
    up_bias,
    down_weight,
    down_bias,
    second_gain,
    second_shift,
    cotangent,
):
    model_width = tokens.shape[1]
    segment_id, usable = layout(lengths[0], tokens.shape[0])
    same_segment = segment_id[:, None] == segment_id[None, :]
    keep_rows = usable.astype(jnp.float32)[:, None]
    w_qkv, b_qv, w_out, b_out, gain_one, shift_one = (
        lax.all_gather(qkv_weight, "shard", axis=0, tiled=True),
        lax.all_gather(qv_bias, "shard", axis=0, tiled=True),
        lax.all_gather(out_weight, "shard", axis=0, tiled=True),
        lax.all_gather(out_bias, "shard", axis=0, tiled=True),
        lax.all_gather(first_gain, "shard", axis=0, tiled=True),
        lax.all_gather(first_shift, "shard", axis=0, tiled=True),
    )
    projected = matmul(tokens, w_qkv)
    bias_full = b_qv.astype(jnp.float32)
    queries = (projected[:, :model_width] + bias_full[:model_width]).astype(jnp.bfloat16)
    key_rows = projected[:, model_width : 2 * model_width].astype(jnp.bfloat16)
    values = (projected[:, 2 * model_width :] + bias_full[model_width:]).astype(jnp.bfloat16)
    context, log_total = attend(queries, key_rows, values, same_segment)
    attn_out = matmul(context, w_out) + b_out.astype(jnp.float32)
    gain_first = gain_one.astype(jnp.float32)
    hidden, normed_one, inverse_one = normalize(
        tokens.astype(jnp.float32) + attn_out, gain_first, shift_one.astype(jnp.float32)
    )
    hidden_low = hidden.astype(jnp.bfloat16)
    w_up, b_up, w_down, b_down, gain_two, shift_two = (
        lax.all_gather(up_weight, "shard", axis=0, tiled=True),
        lax.all_gather(up_bias, "shard", axis=0, tiled=True),
        lax.all_gather(down_weight, "shard", axis=0, tiled=True),
        lax.all_gather(down_bias, "shard", axis=0, tiled=True),
        lax.all_gather(second_gain, "shard", axis=0, tiled=True),
        lax.all_gather(second_shift, "shard", axis=0, tiled=True),
    )
    pre_act = matmul(hidden_low, w_up) + b_up.astype(jnp.float32)
    activated = jax.nn.gelu(pre_act, approximate=False).astype(jnp.bfloat16)
    branch = matmul(activated, w_down) + b_down.astype(jnp.float32)
    gain_second = gain_two.astype(jnp.float32)
    output_full, normed_two, inverse_two = normalize(
        hidden + branch, gain_second, shift_two.astype(jnp.float32)
    )
    layer_out = (output_full * keep_rows).astype(jnp.bfloat16)
    grad_out = cotangent.astype(jnp.float32) * keep_rows
    grad_second, grad_gain_two, grad_shift_two = normalize_back(
        grad_out, normed_two, inverse_two, gain_second
    )
    back_up, back_down = (w_up, w_down)
    grad_branch = grad_second.astype(jnp.bfloat16)
    grad_w_down = matmul_tn(activated, grad_branch)
    grad_b_down = jnp.sum(grad_branch.astype(jnp.float32), axis=0)
    grad_act = matmul_nt(grad_branch, back_down)
    gelu_value, gelu_pull = jax.vjp(partial(jax.nn.gelu, approximate=False), pre_act)
    grad_pre = gelu_pull(grad_act)[0].astype(jnp.bfloat16)
    grad_w_up = matmul_tn(hidden_low, grad_pre)
    grad_b_up = jnp.sum(grad_pre.astype(jnp.float32), axis=0)
    grad_hidden = grad_second + matmul_nt(grad_pre, back_up)
    ffn_shares = (
        lax.psum_scatter(
            grad_w_up.astype(jnp.bfloat16), "shard", scatter_dimension=0, tiled=True
        ).astype(jnp.float32),
        lax.psum_scatter(
            grad_b_up.astype(jnp.bfloat16), "shard", scatter_dimension=0, tiled=True
        ).astype(jnp.float32),
        lax.psum_scatter(
            grad_w_down.astype(jnp.bfloat16), "shard", scatter_dimension=0, tiled=True
        ).astype(jnp.float32),
        lax.psum_scatter(
            grad_b_down.astype(jnp.bfloat16), "shard", scatter_dimension=0, tiled=True
        ).astype(jnp.float32),
        lax.psum_scatter(
            grad_gain_two.astype(jnp.bfloat16), "shard", scatter_dimension=0, tiled=True
        ).astype(jnp.float32),
        lax.psum_scatter(
            grad_shift_two.astype(jnp.bfloat16), "shard", scatter_dimension=0, tiled=True
        ).astype(jnp.float32),
    )
    grad_first, grad_gain_one, grad_shift_one = normalize_back(
        grad_hidden, normed_one, inverse_one, gain_first
    )
    back_qkv, back_out = (w_qkv, w_out)
    grad_attn = grad_first.astype(jnp.bfloat16)
    grad_w_out = matmul_tn(context, grad_attn)
    grad_b_out = jnp.sum(grad_attn.astype(jnp.float32), axis=0)
    grad_context = matmul_nt(grad_attn, back_out).astype(jnp.bfloat16)
    grad_queries, grad_keys, grad_values = attend_back(
        grad_context, queries, key_rows, values, same_segment, log_total
    )
    grad_proj = jnp.concatenate([grad_queries, grad_keys, grad_values], axis=1)
    grad_w_qkv = matmul_tn(tokens, grad_proj)
    grad_b_qv = jnp.concatenate(
        [
            jnp.sum(grad_queries.astype(jnp.float32), axis=0),
            jnp.sum(grad_values.astype(jnp.float32), axis=0),
        ]
    )
    grad_tokens = (grad_first + matmul_nt(grad_proj, back_qkv)).astype(jnp.bfloat16)
    attn_shares = (
        lax.psum_scatter(
            grad_w_qkv.astype(jnp.bfloat16), "shard", scatter_dimension=0, tiled=True
        ).astype(jnp.float32),
        lax.psum_scatter(
            grad_b_qv.astype(jnp.bfloat16), "shard", scatter_dimension=0, tiled=True
        ).astype(jnp.float32),
        lax.psum_scatter(
            grad_w_out.astype(jnp.bfloat16), "shard", scatter_dimension=0, tiled=True
        ).astype(jnp.float32),
        lax.psum_scatter(
            grad_b_out.astype(jnp.bfloat16), "shard", scatter_dimension=0, tiled=True
        ).astype(jnp.float32),
        lax.psum_scatter(
            grad_gain_one.astype(jnp.bfloat16), "shard", scatter_dimension=0, tiled=True
        ).astype(jnp.float32),
        lax.psum_scatter(
            grad_shift_one.astype(jnp.bfloat16), "shard", scatter_dimension=0, tiled=True
        ).astype(jnp.float32),
    )
    totals = (
        lax.psum(ffn_shares[0].astype(jnp.bfloat16), "replica").astype(jnp.float32),
        lax.psum(ffn_shares[1].astype(jnp.bfloat16), "replica").astype(jnp.float32),
        lax.psum(ffn_shares[2].astype(jnp.bfloat16), "replica").astype(jnp.float32),
        lax.psum(ffn_shares[3].astype(jnp.bfloat16), "replica").astype(jnp.float32),
        lax.psum(ffn_shares[4].astype(jnp.bfloat16), "replica").astype(jnp.float32),
        lax.psum(ffn_shares[5].astype(jnp.bfloat16), "replica").astype(jnp.float32),
        lax.psum(attn_shares[0].astype(jnp.bfloat16), "replica").astype(jnp.float32),
        lax.psum(attn_shares[1].astype(jnp.bfloat16), "replica").astype(jnp.float32),
        lax.psum(attn_shares[2].astype(jnp.bfloat16), "replica").astype(jnp.float32),
        lax.psum(attn_shares[3].astype(jnp.bfloat16), "replica").astype(jnp.float32),
        lax.psum(attn_shares[4].astype(jnp.bfloat16), "replica").astype(jnp.float32),
        lax.psum(attn_shares[5].astype(jnp.bfloat16), "replica").astype(jnp.float32),
    )
    return (
        layer_out,
        grad_tokens,
        totals[6],
        totals[7],
        totals[8],
        totals[9],
        totals[10],
        totals[11],
        totals[0],
        totals[1],
        totals[2],
        totals[3],
        totals[4],
        totals[5],
    )


def on_device_direct(
    tokens,
    lengths,
    qkv_weight,
    qv_bias,
    out_weight,
    out_bias,
    first_gain,
    first_shift,
    up_weight,
    up_bias,
    down_weight,
    down_bias,
    second_gain,
    second_shift,
    cotangent,
):
    rows, model_width = tokens.shape
    replica = lax.axis_index("replica").astype(jnp.int32)
    shard = lax.axis_index("shard").astype(jnp.int32)
    x, core, z, y = replica // 2, replica % 2, shard // 2, shard % 2
    position = jnp.stack([replica, shard])
    small = (qv_bias, out_bias, first_gain, first_shift, up_bias, down_bias, second_gain, second_shift)

    def shaped(*shape, dtype=jnp.bfloat16):
        return jax.ShapeDtypeStruct(shape, dtype)

    quarter_attn = jnp.where(
        replica == 3,
        out_weight,
        lax.dynamic_slice_in_dim(qkv_weight, jnp.minimum(replica, 2) * 768, 768, axis=1),
    )
    quarter_up = lax.dynamic_index_in_dim(
        up_weight.reshape(up_weight.shape[0], SHARDS, REPLICAS, -1), replica, 2, False
    ).reshape(-1, 768)
    quarter_down = lax.dynamic_slice_in_dim(down_weight, replica * 96, 96, axis=0)
    z_attn = swap_zs(quarter_attn)
    z_up = swap_zs(after(quarter_up, *z_attn))
    half_attn = halves_of(z_attn)
    first_attn = cross_first(half_attn)
    packed = small_gather(after(jnp.concatenate(small), *first_attn), z, y)
    near_attn = near_of(half_attn, first_attn)
    far_attn = cross_second(near_attn)
    z_down = swap_zs(after(quarter_down, *z_up))
    near_up = jnp.stack(z_up)
    far_up = swap_y(near_up)
    near_down = jnp.stack(z_down)
    far_down = swap_y(near_down)
    core_attn = parts_of(near_attn, far_attn, swap_cores(near_attn), swap_cores(far_attn))
    core_attn = [after(core_attn[0], near_up, near_down)] + core_attn[1:]
    f32 = jnp.float32
    (
        w_attn,
        proj,
        weights,
        context,
        hidden,
        hidden_low,
        normed_one,
        inverse_one,
        table,
        keep,
    ) = kernel_call(
        attend_kernel,
        "attend",
        (
            shaped(768, 3072),
            shaped(rows, 2304),
            shaped(HEADS, rows, rows, dtype=f32),
            shaped(rows, 768),
            shaped(rows, 768, dtype=f32),
            shaped(rows, 768),
            shaped(rows, 768, dtype=f32),
            shaped(rows, 1, dtype=f32),
            shaped(12, 768, dtype=f32),
            shaped(rows, 1, dtype=f32),
        ),
        [position, lengths, tokens, packed] + core_attn,
        scalars=2,
    )
    hidden_blocks = share(after(hidden_low, far_up))
    w_up, w_down, activated, slope, near, far = kernel_call(
        feed_kernel,
        "feed",
        (
            shaped(768, 768),
            shaped(768, 768),
            shaped(4 * rows, 768),
            shaped(4 * rows, 768, dtype=f32),
            shaped(2, rows, 768),
            shaped(2, rows, 768),
        ),
        [position, *hidden_blocks, table, near_up, far_up, near_down, far_down],
    )
    mine, come = collect(near, far)
    layer_out, grad_second, grad_branch, small_down = kernel_call(
        close_kernel,
        "close",
        (
            shaped(rows, 768),
            shaped(rows, 768, dtype=f32),
            shaped(rows, 768),
            shaped(3, 768, dtype=f32),
        ),
        [position, mine, come, hidden, table, keep, cotangent],
    )
    grad_blocks = share(grad_branch)
    grad_pre, near, far, grad_b_quarter = kernel_call(
        back_kernel,
        "back",
        (
            shaped(4 * rows, 768),
            shaped(2, rows, 768),
            shaped(2, rows, 768),
            shaped(1, 768, dtype=f32),
        ),
        [position, *grad_blocks, slope, w_up, w_down],
    )
    block = shaped(4, 96, 768)
    total = [pltpu.VMEM((768, 768), jnp.bfloat16)]
    near_up, far_up = kernel_call(
        partial(weight_kernel, 4),
        "grad_up",
        (block, block),
        [position, *hidden_blocks, grad_pre],
        total,
    )
    near_down, far_down = kernel_call(
        partial(weight_kernel, 1),
        "grad_down",
        (block, block),
        [position, activated, *grad_blocks],
        total,
    )
    come_up = swap_y(far_up)
    come_down = swap_y(after(far_down, come_up))
    last_up = plus(near_up, come_up)
    zs_up = send_zs(last_up)
    mine, come = collect(near, far)
    outs = kernel_call(
        attend_back_kernel,
        "attend_back",
        tuple(shaped(2, 4, 48, 768) for _ in range(8))
        + (
            shaped(rows, 768, dtype=f32),
            shaped(rows, 2304),
            shaped(5, 768, dtype=f32),
        ),
        [position, mine, come, grad_second, normed_one, inverse_one, table]
        + [context, proj, weights, w_attn, tokens],
        [pltpu.VMEM((768, 3072), jnp.bfloat16)],
    )
    parts_attn = outs[:8]
    grad_first, grad_proj, small_attn = outs[8:]
    last_down = plus(near_down, come_down)
    zs_down = send_zs(last_down)
    far, near = sum_parts(parts_attn, swap_parts(parts_attn))
    (grad_tokens,) = kernel_call(
        tokens_kernel,
        "grad_tokens",
        (shaped(rows, 768),),
        [position, after(grad_first, *far), grad_proj, w_attn],
    )
    small_attn = after(small_attn, *far)
    small_total = small_sum(
        jnp.concatenate(
            [
                small_attn,
                jnp.where(jnp.arange(REPLICAS)[:, None] == replica, grad_b_quarter, 0.0),
                small_down,
            ]
        )
    )
    near[0] = after(near[0], *zs_down)
    onward, stay_attn = sum_plane(near, cross_second(far))
    last_attn = sum_last(stay_attn, cross_first(onward))
    zs_attn = send_zs(last_attn)
    reduced_up = after(sum_zs(last_up, zs_up), *onward)
    reduced_down = after(sum_zs(last_down, zs_down), *onward)
    reduced_attn = sum_zs(last_attn, zs_attn)
    d_down = spread(reduced_down, x, core).reshape(-1, 768).astype(f32)
    up_quarters = spread(reduced_up, x, core).astype(f32)
    d_up = jnp.stack(
        [up_quarters[at].reshape(-1, SHARDS, 96) for at in range(REPLICAS)], axis=2
    ).reshape(-1, 3072)
    attn_quarters = spread(reduced_attn, x, core).astype(f32)
    d_qkv = jnp.concatenate([attn_quarters[at] for at in range(3)], axis=1)
    d_out = attn_quarters[3]
    d_qv_bias = lax.dynamic_slice_in_dim(small_total[:2].reshape(-1), shard * 192, 192)
    mine = lax.dynamic_slice_in_dim(small_total[2:], shard * 96, 96, axis=1)
    return (
        layer_out,
        grad_tokens,
        d_qkv,
        d_qv_bias,
        d_out,
        mine[0],
        mine[1],
        mine[2],
        d_up,
        mine[3:7].reshape(-1),
        d_down,
        mine[7],
        mine[8],
        mine[9],
    )


def solution(mesh):
    shape = dict(mesh.shape)
    direct = shape["replica"] == REPLICAS and shape["shard"] == SHARDS
    placed = (
        P(("replica", "shard"), None),
        P(("replica", "shard"), None),
        P("shard", None),
        P("shard"),
        P("shard", None),
        P("shard"),
        P("shard"),
        P("shard"),
        P("shard", None),
        P("shard"),
        P("shard", None),
        P("shard"),
        P("shard"),
        P("shard"),
        P(("replica", "shard"), None),
    )
    return jax.shard_map(
        on_device_direct if direct else on_device_general,
        mesh=mesh,
        in_specs=placed,
        out_specs=(
            P(("replica", "shard"), None),
            P(("replica", "shard"), None),
            P("shard", None),
            P("shard"),
            P("shard", None),
            P("shard"),
            P("shard"),
            P("shard"),
            P("shard", None),
            P("shard"),
            P("shard", None),
            P("shard"),
            P("shard"),
            P("shard"),
        ),
        check_vma=False,
    )
```

```python
from functools import partial

import jax
import jax.numpy as jnp
from jax import lax
from jax.experimental import pallas as pl
from jax.experimental.pallas import tpu as pltpu
from jax.sharding import PartitionSpec as P

HEADS = 12


EPSILON = 1e-05
NEG_FILL = -1e30


def layout(length_row, row_count):
    bounds = jnp.cumsum(length_row)
    places = jnp.arange(row_count, dtype=jnp.int32)
    segment = jnp.sum((places[:, None] >= bounds[None, :]).astype(jnp.int32), axis=1)
    usable = places < bounds[-1]
    segment_id = jnp.where(usable, segment, length_row.shape[0] + places)
    return (segment_id, usable)


def matmul(left_side, right_side):
    return jnp.dot(left_side, right_side, preferred_element_type=jnp.float32)


def matmul_tn(left_side, right_side):
    return lax.dot_general(
        left_side, right_side, (((0,), (0,)), ((), ())), preferred_element_type=jnp.float32
    )


def matmul_nt(left_side, right_side):
    return lax.dot_general(
        left_side, right_side, (((1,), (1,)), ((), ())), preferred_element_type=jnp.float32
    )


def normalize(residual, norm_gain, norm_shift):
    center = residual - jnp.mean(residual, axis=1, keepdims=True)
    inverse = lax.rsqrt(jnp.mean(center * center, axis=1, keepdims=True) + EPSILON)
    normed = center * inverse
    return (normed * norm_gain + norm_shift, normed, inverse)


def normalize_back(grad_out, normed, inverse, norm_gain):
    scaled = grad_out * norm_gain
    grad_in = inverse * (
        scaled
        - jnp.mean(scaled, axis=1, keepdims=True)
        - normed * jnp.mean(scaled * normed, axis=1, keepdims=True)
    )
    return (grad_in, jnp.sum(grad_out * normed, axis=0), jnp.sum(grad_out, axis=0))


def split_heads(tensor):
    return tensor.reshape((tensor.shape[0], HEADS, tensor.shape[1] // HEADS))


def masked_scores(queries, key_rows, same_segment):
    scale_factor = (queries.shape[1] // HEADS) ** (-0.5)
    scores = (
        jnp.einsum(
            "qhd,khd->hqk",
            split_heads(queries),
            split_heads(key_rows),
            preferred_element_type=jnp.float32,
        )
        * scale_factor
    )
    return jnp.where(same_segment[None], scores, NEG_FILL)


def attend(queries, key_rows, values, same_segment):
    masked = masked_scores(queries, key_rows, same_segment)
    highest = jnp.max(masked, axis=2, keepdims=True)
    weights = jnp.exp(masked - highest)
    total = jnp.sum(weights, axis=2, keepdims=True)
    log_total = highest + jnp.log(total)
    attn_probs = (weights / total).astype(jnp.bfloat16)
    context = jnp.einsum(
        "hqk,khd->qhd", attn_probs, split_heads(values), preferred_element_type=jnp.float32
    )
    return (context.reshape(queries.shape).astype(jnp.bfloat16), log_total)


def attend_back(grad_context, queries, key_rows, values, same_segment, log_total):
    scale_factor = (queries.shape[1] // HEADS) ** (-0.5)
    masked = masked_scores(queries, key_rows, same_segment)
    attn_probs = jnp.exp(masked - log_total)
    probs_low = attn_probs.astype(jnp.bfloat16)
    grad_heads = split_heads(grad_context)
    grad_probs = jnp.einsum(
        "qhd,khd->hqk", grad_heads, split_heads(values), preferred_element_type=jnp.float32
    )
    grad_values = jnp.einsum(
        "hqk,qhd->khd", probs_low, grad_heads, preferred_element_type=jnp.float32
    )
    inner = jnp.sum(attn_probs * grad_probs, axis=2, keepdims=True)
    grad_scores = (attn_probs * (grad_probs - inner)).astype(jnp.bfloat16)
    grad_queries = (
        jnp.einsum(
            "hqk,khd->qhd", grad_scores, split_heads(key_rows), preferred_element_type=jnp.float32
        )
        * scale_factor
    )
    grad_keys = (
        jnp.einsum(
            "hqk,qhd->khd", grad_scores, split_heads(queries), preferred_element_type=jnp.float32
        )
        * scale_factor
    )
    shape_flat = queries.shape
    return (
        grad_queries.reshape(shape_flat).astype(jnp.bfloat16),
        grad_keys.reshape(shape_flat).astype(jnp.bfloat16),
        grad_values.reshape(shape_flat).astype(jnp.bfloat16),
    )


AXES = ("replica", "shard")
REPLICAS = 4
SHARDS = 8


def swap_pairs(dx, dcore, dz, dy):
    pairs = []
    for replica in range(REPLICAS):
        for shard in range(SHARDS):
            to_replica = replica ^ (dx * 2 + dcore)
            to_shard = shard ^ (dz * 2 + dy)
            pairs.append((replica * SHARDS + shard, to_replica * SHARDS + to_shard))
    return pairs


def swap_x(value):
    return lax.ppermute(value, AXES, swap_pairs(1, 0, 0, 0))


def swap_core(value):
    return lax.ppermute(value, AXES, swap_pairs(0, 1, 0, 0))


def swap_y(value):
    return lax.ppermute(value, AXES, swap_pairs(0, 0, 0, 1))


def swap_z(value, distance):
    return lax.ppermute(value, AXES, swap_pairs(0, 0, distance, 0))


def together(*trees):
    return lax.optimization_barrier(trees)


def share(block):
    across = swap_x(block)
    return [block, swap_core(block), across, swap_core(across)]


def collect(near, far):
    pair = plus(near, swap_core(far))
    return pair[0], swap_x(pair[1])


def swap_zs(piece):
    return [piece] + [swap_z(piece, distance) for distance in (1, 2, 3)]


def halves_of(pieces):
    half = pieces[0].shape[0] // 2
    return [jnp.stack([entry[at : at + half] for entry in pieces]) for at in (0, half)]


def cross_first(halves):
    return [swap_y(halves[0]), swap_x(halves[1])]


def near_of(halves, come):
    return [jnp.stack(pair) for pair in zip(halves, come)]


def cross_second(near):
    return [swap_x(near[0]), swap_y(near[1])]


def swap_cores(parts):
    return [swap_core(entry) for entry in parts]


def parts_of(near, far, core_near, core_far):
    return [entry for group in zip(near, far, core_near, core_far) for entry in group]


def route(leading, start, rows):
    return [(leading, fixed, core, start, rows) for core in range(2) for fixed in range(2)]


PLAN = route("y", 0, 48) + route("x", 48, 48)


def plus(left_side, right_side):
    return (left_side.astype(jnp.float32) + right_side.astype(jnp.float32)).astype(jnp.bfloat16)


def swap_parts(parts):
    return [swap_core(parts[at]) for at in (3, 7, 2, 6)]


def sum_parts(parts, come):
    far = [plus(parts[1], come[0]), plus(parts[5], come[1])]
    return far, [plus(parts[0], come[2]), plus(parts[4], come[3])]


def sum_plane(near, come):
    onward = [plus(mine[1], other[1]) for mine, other in zip(near, come)]
    return onward, [plus(mine[0], other[0]) for mine, other in zip(near, come)]


def sum_last(stay, come):
    return jnp.concatenate([plus(mine, other) for mine, other in zip(stay, come)], axis=1)


def send_zs(block):
    return [swap_z(block[distance], distance) for distance in (1, 2, 3)]


def sum_zs(block, come):
    total = block[0].astype(jnp.float32)
    for entry in come:
        total = total + entry.astype(jnp.float32)
    return total.astype(jnp.bfloat16)


KERNEL_VMEM = 10 * 2**20
ROOT_HALF = 0.7071067811865476
ROOT_TWO_PI = 0.3989422804014327
VMEM = pl.BlockSpec(memory_space=pltpu.VMEM)
SMEM = pl.BlockSpec(memory_space=pltpu.SMEM)
ROWS_OF = (2, 1, 1, 1, 4, 1, 1, 1)


def kernel_call(kernel, name, out_shapes, inputs, scratch=(), scalars=1, behind=()):
    count = len(inputs)

    def body(*refs):
        kernel(*refs[:count], *refs[count + len(behind) :])

    return pl.pallas_call(
        body,
        out_shape=tuple(out_shapes),
        in_specs=[SMEM] * scalars
        + [VMEM] * (count - scalars)
        + [pl.BlockSpec(memory_space=pl.ANY)] * len(behind),
        out_specs=(VMEM,) * len(out_shapes),
        scratch_shapes=list(scratch),
        compiler_params=pltpu.CompilerParams(vmem_limit_bytes=KERNEL_VMEM),
        cost_estimate=pl.CostEstimate(flops=2**20, bytes_accessed=2**20, transcendentals=0),
        name=name,
    )(*inputs, *behind)


def places(replica, shard):
    for at, (leading, fixed, core, start, count) in enumerate(PLAN):
        for first in range(2):
            x, y = (first, fixed) if leading == "x" else (fixed, first)
            columns = pl.ds(pl.multiple_of((replica ^ (x * 2 + core)) * 768, 128), 768)
            for z in range(4):
                owner = shard ^ (z * 2 + y)
                rows = pl.ds(pl.multiple_of(owner * 96 + start, 16), count)
                yield at, first, z, rows, columns


def segments(lengths, dim, shape):
    at = lax.broadcasted_iota(jnp.int32, shape, dim)
    bound = jnp.int32(0)
    segment = jnp.zeros(shape, jnp.int32)
    for sequence in range(lengths.shape[1]):
        bound = bound + lengths[0, sequence]
        segment = segment + (at >= bound).astype(jnp.int32)
    return jnp.where(at < bound, segment, lengths.shape[1] + at), at < bound


def head_masks(width):
    lane = lax.broadcasted_iota(jnp.int32, (1, width), 1)
    low = lane < width // 2
    return low, [low.astype(jnp.bfloat16), 1.0 - low.astype(jnp.bfloat16)]


def attend_kernel(position, lengths, tokens, packed, *refs):
    parts, refs = refs[:8], refs[8:]
    whole, w_out, proj, weights, context, hidden, hidden_low, normed_one = refs[:8]
    inverse_one, table, keep = refs[8:]
    for at, first, z, rows, columns in places(position[0], position[1]):
        whole[rows, columns] = parts[at][first, z]
    w_out[...] = whole[:, 2304:]
    pieces = packed[...].astype(jnp.float32)
    row, column = 0, 0
    for count in ROWS_OF:
        for at in range(count):
            if count == 2:
                owners = range(at * 4, at * 4 + 4)
                values = [pieces[owner : owner + 1, 0:192] for owner in owners]
            else:
                start = column + at * 96
                values = [pieces[owner : owner + 1, start : start + 96] for owner in range(SHARDS)]
            table[row : row + 1, :] = jnp.concatenate(values, axis=1)
            row += 1
        column += count * 96
    for step in range(3):
        columns = slice(step * 768, (step + 1) * 768)
        projected = matmul(tokens[...], whole[:, columns])
        if step == 0:
            projected = projected + table[0:1, :]
        if step == 2:
            projected = projected + table[1:2, :]
        proj[:, columns] = projected.astype(jnp.bfloat16)
    count = tokens.shape[0]
    across, usable = segments(lengths, 0, (count, 1))
    along, _ = segments(lengths, 1, (1, count))
    keep[...] = usable.astype(jnp.float32)
    same = across == along
    low, masks = head_masks(128)
    for pair in range(HEADS // 2):
        queries, key_rows, values = (
            proj[:, step * 768 + pair * 128 : step * 768 + (pair + 1) * 128] for step in range(3)
        )
        sums = []
        for which in range(2):
            scores = matmul_nt(queries * masks[which], key_rows) * 0.125
            masked = jnp.where(same, scores, NEG_FILL)
            entries = jnp.exp(masked - jnp.max(masked, axis=1, keepdims=True))
            share_of = entries / jnp.sum(entries, axis=1, keepdims=True)
            weights[pair * 2 + which] = share_of
            sums.append(matmul(share_of.astype(jnp.bfloat16), values))
        context[:, pair * 128 : (pair + 1) * 128] = jnp.where(low, sums[0], sums[1]).astype(
            jnp.bfloat16
        )
    attn_out = matmul(context[...], whole[:, 2304:]) + table[2:3, :]
    result, normed, inverse = normalize(
        tokens[...].astype(jnp.float32) + attn_out, table[3:4, :], table[4:5, :]
    )
    hidden[...] = result
    hidden_low[...] = result.astype(jnp.bfloat16)
    normed_one[...] = normed
    inverse_one[...] = inverse


def column_sum(values):
    return jnp.sum(values.astype(jnp.float32), axis=0, keepdims=True)


def attend_back_kernel(
    position,
    mine,
    come,
    grad_second,
    normed_one,
    inverse_one,
    table,
    context,
    proj,
    weights,
    w_out,
    tokens,
    *refs,
):
    parts, refs = refs[:8], refs[8:]
    grad_first, grad_proj, small, total = refs
    grad_hidden = grad_second[...] + (mine[...].astype(jnp.float32) + come[...].astype(jnp.float32))
    grad_in, grad_gain, grad_shift = normalize_back(
        grad_hidden, normed_one[...], inverse_one[...], table[3:4, :]
    )
    grad_first[...] = grad_in
    grad_attn = grad_in.astype(jnp.bfloat16)
    small[2:3, :] = column_sum(grad_attn)
    small[3:4, :] = grad_gain[None, :]
    small[4:5, :] = grad_shift[None, :]
    total[:, 2304:] = matmul_tn(context[...], grad_attn).astype(jnp.bfloat16)
    grad_context = matmul_nt(grad_attn, w_out[...]).astype(jnp.bfloat16)
    low, masks = head_masks(128)
    for pair in range(HEADS // 2):
        queries, key_rows, values = (
            proj[:, step * 768 + pair * 128 : step * 768 + (pair + 1) * 128] for step in range(3)
        )
        grad_pair = grad_context[:, pair * 128 : (pair + 1) * 128]
        sums = []
        for which in range(2):
            share_of = weights[pair * 2 + which]
            grad_probs = matmul_nt(grad_pair * masks[which], values)
            inner = jnp.sum(share_of * grad_probs, axis=1, keepdims=True)
            grad_scores = (share_of * (grad_probs - inner)).astype(jnp.bfloat16)
            sums.append(
                (
                    matmul(grad_scores, key_rows) * 0.125,
                    matmul_tn(grad_scores, queries) * 0.125,
                    matmul_tn(share_of.astype(jnp.bfloat16), grad_pair),
                )
            )
        for step in range(3):
            grad_proj[:, step * 768 + pair * 128 : step * 768 + (pair + 1) * 128] = jnp.where(
                low, sums[0][step], sums[1][step]
            ).astype(jnp.bfloat16)
    for step in range(3):
        columns = slice(step * 768, (step + 1) * 768)
        total[:, columns] = matmul_tn(tokens[...], grad_proj[:, columns]).astype(jnp.bfloat16)
    small[0:1, :] = column_sum(grad_proj[:, :768])
    small[1:2, :] = column_sum(grad_proj[:, 1536:])
    for at, first, z, rows, columns in places(position[0], position[1]):
        parts[at][first, z] = total[rows, columns]


def tokens_kernel(position, grad_first, grad_proj, whole, grad_tokens):
    grad_tokens[...] = (grad_first[...] + matmul_nt(grad_proj[...], whole[:, :2304])).astype(
        jnp.bfloat16
    )


def blocks_of(near, far, shard):
    for y, part in enumerate((near, far)):
        for z in range(4):
            owner = shard ^ (z * 2 + y)
            yield part, z, pl.ds(pl.multiple_of(owner * 96, 16), 96)


def feed_kernel(
    position, own, from_core, from_x, from_both, table, quarter_near, quarter_far, *outs
):
    w_up, w_down, activated, slope, near, far = outs
    for part, z, rows in blocks_of(quarter_near, quarter_far, position[1]):
        w_up[rows, :] = part[z, :96]
        w_down[rows, :] = part[z, 96:]
    bias = table[pl.ds(5 + position[0], 1), :]
    spots = ((near, 0), (far, 0), (near, 1), (far, 1))
    for step, block in enumerate((own, from_core, from_x, from_both)):
        rows = slice(step * 128, (step + 1) * 128)
        pre_act = matmul(block[...], w_up[...]) + bias
        below = 0.5 * (1.0 + lax.erf(pre_act * ROOT_HALF))
        active = (pre_act * below).astype(jnp.bfloat16)
        activated[rows, :] = active
        slope[rows, :] = below + pre_act * (ROOT_TWO_PI * jnp.exp(-0.5 * pre_act * pre_act))
        out, at = spots[step]
        out[at] = matmul(active, w_down[...]).astype(jnp.bfloat16)


def close_kernel(position, mine, come, hidden, table, keep, cotangent, *outs):
    layer_out, grad_second, grad_branch, small = outs
    gain = table[10:11, :]
    branch = mine[...].astype(jnp.float32) + come[...].astype(jnp.float32) + table[9:10, :]
    output_full, normed, inverse = normalize(hidden[...] + branch, gain, table[11:12, :])
    layer_out[...] = (output_full * keep[...]).astype(jnp.bfloat16)
    grad_out = cotangent[...].astype(jnp.float32) * keep[...]
    grad_in, grad_gain, grad_shift = normalize_back(grad_out, normed, inverse, gain)
    low_grad = grad_in.astype(jnp.bfloat16)
    grad_second[...] = grad_in
    grad_branch[...] = low_grad
    small[0:1, :] = jnp.sum(low_grad.astype(jnp.float32), axis=0, keepdims=True)
    small[1:2, :] = grad_gain[None, :]
    small[2:3, :] = grad_shift[None, :]


def back_kernel(position, own, from_core, from_x, from_both, slope, w_up, w_down, *outs):
    grad_pre, near, far, small = outs
    spots = ((near, 0), (far, 0), (near, 1), (far, 1))
    total = jnp.zeros((1, slope.shape[1]), jnp.float32)
    for step, block in enumerate((own, from_core, from_x, from_both)):
        rows = slice(step * 128, (step + 1) * 128)
        grad = matmul_nt(block[...], w_down[...]) * slope[rows, :]
        low_grad = grad.astype(jnp.bfloat16)
        grad_pre[rows, :] = low_grad
        total = total + jnp.sum(low_grad.astype(jnp.float32), axis=0, keepdims=True)
        out, at = spots[step]
        out[at] = matmul_nt(low_grad, w_up[...]).astype(jnp.bfloat16)
    small[...] = total


def weight_kernel(position, activated, grad_pre, *refs):
    hidden_blocks, grad_blocks, (near, far, up, down) = refs[:4], refs[4:8], refs[8:]
    up[...] = matmul_tn(joined(hidden_blocks), grad_pre[...]).astype(jnp.bfloat16)
    down[...] = matmul_tn(activated[...], joined(grad_blocks)).astype(jnp.bfloat16)
    for part, z, rows in blocks_of(near, far, position[1]):
        part[z, :96] = up[rows, :]
        part[z, 96:] = down[rows, :]


def order(position, mine, across, other, blocks):
    replica = position[0]
    blocks[replica] = mine[...]
    blocks[replica ^ 2] = across[...]
    blocks[replica ^ 1] = other[0]
    blocks[replica ^ 3] = other[1]


def finish_feed_kernel(position, mine, across, other, grad_up, grad_down, blocks):
    order(position, mine, across, other, blocks)
    for quarter in range(REPLICAS):
        grad_down[quarter * 96 : (quarter + 1) * 96, :] = blocks[quarter, 96:].astype(jnp.float32)
    for owner in range(SHARDS):
        grad_up[:, owner * 384 : (owner + 1) * 384] = jnp.concatenate(
            [
                blocks[quarter, :96, owner * 96 : (owner + 1) * 96].astype(jnp.float32)
                for quarter in range(REPLICAS)
            ],
            axis=1,
        )


def finish_attend_kernel(position, mine, across, other, grad_qkv, grad_out, blocks):
    order(position, mine, across, other, blocks)
    for quarter in range(3):
        grad_qkv[:, quarter * 768 : (quarter + 1) * 768] = blocks[quarter].astype(jnp.float32)
    grad_out[...] = blocks[3].astype(jnp.float32)


def joined(refs):
    return jnp.concatenate([entry[...] for entry in refs], axis=0)


def small_gather(vector, z, y):
    block = vector[None]
    other = swap_y(block)
    block = jnp.concatenate([jnp.where(y == 0, block, other), jnp.where(y == 0, other, block)])
    for distance in (1, 2):
        other = swap_z(block, distance)
        low_side = (z & distance) == 0
        block = jnp.concatenate(
            [jnp.where(low_side, block, other), jnp.where(low_side, other, block)]
        )
    return block


def on_device_general(
    tokens,
    lengths,
    qkv_weight,
    qv_bias,
    out_weight,
    out_bias,
    first_gain,
    first_shift,
    up_weight,
    up_bias,
    down_weight,
    down_bias,
    second_gain,
    second_shift,
    cotangent,
):
    model_width = tokens.shape[1]
    segment_id, usable = layout(lengths[0], tokens.shape[0])
    same_segment = segment_id[:, None] == segment_id[None, :]
    keep_rows = usable.astype(jnp.float32)[:, None]
    w_qkv, b_qv, w_out, b_out, gain_one, shift_one = (
        lax.all_gather(qkv_weight, "shard", axis=0, tiled=True),
        lax.all_gather(qv_bias, "shard", axis=0, tiled=True),
        lax.all_gather(out_weight, "shard", axis=0, tiled=True),
        lax.all_gather(out_bias, "shard", axis=0, tiled=True),
        lax.all_gather(first_gain, "shard", axis=0, tiled=True),
        lax.all_gather(first_shift, "shard", axis=0, tiled=True),
    )
    projected = matmul(tokens, w_qkv)
    bias_full = b_qv.astype(jnp.float32)
    queries = (projected[:, :model_width] + bias_full[:model_width]).astype(jnp.bfloat16)
    key_rows = projected[:, model_width : 2 * model_width].astype(jnp.bfloat16)
    values = (projected[:, 2 * model_width :] + bias_full[model_width:]).astype(jnp.bfloat16)
    context, log_total = attend(queries, key_rows, values, same_segment)
    attn_out = matmul(context, w_out) + b_out.astype(jnp.float32)
    gain_first = gain_one.astype(jnp.float32)
    hidden, normed_one, inverse_one = normalize(
        tokens.astype(jnp.float32) + attn_out, gain_first, shift_one.astype(jnp.float32)
    )
    hidden_low = hidden.astype(jnp.bfloat16)
    w_up, b_up, w_down, b_down, gain_two, shift_two = (
        lax.all_gather(up_weight, "shard", axis=0, tiled=True),
        lax.all_gather(up_bias, "shard", axis=0, tiled=True),
        lax.all_gather(down_weight, "shard", axis=0, tiled=True),
        lax.all_gather(down_bias, "shard", axis=0, tiled=True),
        lax.all_gather(second_gain, "shard", axis=0, tiled=True),
        lax.all_gather(second_shift, "shard", axis=0, tiled=True),
    )
    pre_act = matmul(hidden_low, w_up) + b_up.astype(jnp.float32)
    activated = jax.nn.gelu(pre_act, approximate=False).astype(jnp.bfloat16)
    branch = matmul(activated, w_down) + b_down.astype(jnp.float32)
    gain_second = gain_two.astype(jnp.float32)
    output_full, normed_two, inverse_two = normalize(
        hidden + branch, gain_second, shift_two.astype(jnp.float32)
    )
    layer_out = (output_full * keep_rows).astype(jnp.bfloat16)
    grad_out = cotangent.astype(jnp.float32) * keep_rows
    grad_second, grad_gain_two, grad_shift_two = normalize_back(
        grad_out, normed_two, inverse_two, gain_second
    )
    back_up, back_down = (w_up, w_down)
    grad_branch = grad_second.astype(jnp.bfloat16)
    grad_w_down = matmul_tn(activated, grad_branch)
    grad_b_down = jnp.sum(grad_branch.astype(jnp.float32), axis=0)
    grad_act = matmul_nt(grad_branch, back_down)
    gelu_value, gelu_pull = jax.vjp(partial(jax.nn.gelu, approximate=False), pre_act)
    grad_pre = gelu_pull(grad_act)[0].astype(jnp.bfloat16)
    grad_w_up = matmul_tn(hidden_low, grad_pre)
    grad_b_up = jnp.sum(grad_pre.astype(jnp.float32), axis=0)
    grad_hidden = grad_second + matmul_nt(grad_pre, back_up)
    ffn_shares = (
        lax.psum_scatter(
            grad_w_up.astype(jnp.bfloat16), "shard", scatter_dimension=0, tiled=True
        ).astype(jnp.float32),
        lax.psum_scatter(
            grad_b_up.astype(jnp.bfloat16), "shard", scatter_dimension=0, tiled=True
        ).astype(jnp.float32),
        lax.psum_scatter(
            grad_w_down.astype(jnp.bfloat16), "shard", scatter_dimension=0, tiled=True
        ).astype(jnp.float32),
        lax.psum_scatter(
            grad_b_down.astype(jnp.bfloat16), "shard", scatter_dimension=0, tiled=True
        ).astype(jnp.float32),
        lax.psum_scatter(
            grad_gain_two.astype(jnp.bfloat16), "shard", scatter_dimension=0, tiled=True
        ).astype(jnp.float32),
        lax.psum_scatter(
            grad_shift_two.astype(jnp.bfloat16), "shard", scatter_dimension=0, tiled=True
        ).astype(jnp.float32),
    )
    grad_first, grad_gain_one, grad_shift_one = normalize_back(
        grad_hidden, normed_one, inverse_one, gain_first
    )
    back_qkv, back_out = (w_qkv, w_out)
    grad_attn = grad_first.astype(jnp.bfloat16)
    grad_w_out = matmul_tn(context, grad_attn)
    grad_b_out = jnp.sum(grad_attn.astype(jnp.float32), axis=0)
    grad_context = matmul_nt(grad_attn, back_out).astype(jnp.bfloat16)
    grad_queries, grad_keys, grad_values = attend_back(
        grad_context, queries, key_rows, values, same_segment, log_total
    )
    grad_proj = jnp.concatenate([grad_queries, grad_keys, grad_values], axis=1)
    grad_w_qkv = matmul_tn(tokens, grad_proj)
    grad_b_qv = jnp.concatenate(
        [
            jnp.sum(grad_queries.astype(jnp.float32), axis=0),
            jnp.sum(grad_values.astype(jnp.float32), axis=0),
        ]
    )
    grad_tokens = (grad_first + matmul_nt(grad_proj, back_qkv)).astype(jnp.bfloat16)
    attn_shares = (
        lax.psum_scatter(
            grad_w_qkv.astype(jnp.bfloat16), "shard", scatter_dimension=0, tiled=True
        ).astype(jnp.float32),
        lax.psum_scatter(
            grad_b_qv.astype(jnp.bfloat16), "shard", scatter_dimension=0, tiled=True
        ).astype(jnp.float32),
        lax.psum_scatter(
            grad_w_out.astype(jnp.bfloat16), "shard", scatter_dimension=0, tiled=True
        ).astype(jnp.float32),
        lax.psum_scatter(
            grad_b_out.astype(jnp.bfloat16), "shard", scatter_dimension=0, tiled=True
        ).astype(jnp.float32),
        lax.psum_scatter(
            grad_gain_one.astype(jnp.bfloat16), "shard", scatter_dimension=0, tiled=True
        ).astype(jnp.float32),
        lax.psum_scatter(
            grad_shift_one.astype(jnp.bfloat16), "shard", scatter_dimension=0, tiled=True
        ).astype(jnp.float32),
    )
    totals = (
        lax.psum(ffn_shares[0].astype(jnp.bfloat16), "replica").astype(jnp.float32),
        lax.psum(ffn_shares[1].astype(jnp.bfloat16), "replica").astype(jnp.float32),
        lax.psum(ffn_shares[2].astype(jnp.bfloat16), "replica").astype(jnp.float32),
        lax.psum(ffn_shares[3].astype(jnp.bfloat16), "replica").astype(jnp.float32),
        lax.psum(ffn_shares[4].astype(jnp.bfloat16), "replica").astype(jnp.float32),
        lax.psum(ffn_shares[5].astype(jnp.bfloat16), "replica").astype(jnp.float32),
        lax.psum(attn_shares[0].astype(jnp.bfloat16), "replica").astype(jnp.float32),
        lax.psum(attn_shares[1].astype(jnp.bfloat16), "replica").astype(jnp.float32),
        lax.psum(attn_shares[2].astype(jnp.bfloat16), "replica").astype(jnp.float32),
        lax.psum(attn_shares[3].astype(jnp.bfloat16), "replica").astype(jnp.float32),
        lax.psum(attn_shares[4].astype(jnp.bfloat16), "replica").astype(jnp.float32),
        lax.psum(attn_shares[5].astype(jnp.bfloat16), "replica").astype(jnp.float32),
    )
    return (
        layer_out,
        grad_tokens,
        totals[6],
        totals[7],
        totals[8],
        totals[9],
        totals[10],
        totals[11],
        totals[0],
        totals[1],
        totals[2],
        totals[3],
        totals[4],
        totals[5],
    )


def on_device_direct(
    tokens,
    lengths,
    qkv_weight,
    qv_bias,
    out_weight,
    out_bias,
    first_gain,
    first_shift,
    up_weight,
    up_bias,
    down_weight,
    down_bias,
    second_gain,
    second_shift,
    cotangent,
):
    rows, model_width = tokens.shape
    replica = lax.axis_index("replica").astype(jnp.int32)
    shard = lax.axis_index("shard").astype(jnp.int32)
    z, y = shard // 2, shard % 2
    position = jnp.stack([replica, shard])
    small = (qv_bias, out_bias, first_gain, first_shift, up_bias, down_bias, second_gain, second_shift)

    def shaped(*shape, dtype=jnp.bfloat16):
        return jax.ShapeDtypeStruct(shape, dtype)

    quarter_attn = jnp.where(
        replica == 3,
        out_weight,
        lax.dynamic_slice_in_dim(qkv_weight, jnp.minimum(replica, 2) * 768, 768, axis=1),
    )
    quarter_up = lax.dynamic_index_in_dim(
        up_weight.reshape(up_weight.shape[0], SHARDS, REPLICAS, -1), replica, 2, False
    ).reshape(-1, 768)
    quarter_down = lax.dynamic_slice_in_dim(down_weight, replica * 96, 96, axis=0)
    z_attn = swap_zs(quarter_attn)
    packed = small_gather(jnp.concatenate(small), z, y)
    quarter_feed = jnp.concatenate([quarter_up, quarter_down])
    z_attn, quarter_feed = together(z_attn, quarter_feed)
    z_feed = swap_zs(quarter_feed)
    half_attn = halves_of(z_attn)
    near_attn = near_of(half_attn, cross_first(half_attn))
    far_attn = cross_second(near_attn)
    far_attn, near_attn, packed = together(far_attn, near_attn, packed)
    core_attn = parts_of(near_attn, far_attn, swap_cores(near_attn), swap_cores(far_attn))
    near_feed = jnp.stack(z_feed)
    far_feed = swap_y(near_feed)
    f32 = jnp.float32
    (
        w_attn,
        w_out,
        proj,
        weights,
        context,
        hidden,
        hidden_low,
        normed_one,
        inverse_one,
        table,
        keep,
    ) = kernel_call(
        attend_kernel,
        "attend",
        (
            shaped(768, 3072),
            shaped(768, 768),
            shaped(rows, 2304),
            shaped(HEADS, rows, rows, dtype=f32),
            shaped(rows, 768),
            shaped(rows, 768, dtype=f32),
            shaped(rows, 768),
            shaped(rows, 768, dtype=f32),
            shaped(rows, 1, dtype=f32),
            shaped(12, 768, dtype=f32),
            shaped(rows, 1, dtype=f32),
        ),
        [position, lengths, tokens, packed] + core_attn,
        scalars=2,
        behind=(near_feed,),
    )
    hidden_blocks = share(hidden_low)
    w_up, w_down, activated, slope, near, far = kernel_call(
        feed_kernel,
        "feed",
        (
            shaped(768, 768),
            shaped(768, 768),
            shaped(4 * rows, 768),
            shaped(4 * rows, 768, dtype=f32),
            shaped(2, rows, 768),
            shaped(2, rows, 768),
        ),
        [position, *hidden_blocks, table, near_feed, far_feed],
    )
    mine, come = collect(near, far)
    layer_out, grad_second, grad_branch, small_down = kernel_call(
        close_kernel,
        "close",
        (
            shaped(rows, 768),
            shaped(rows, 768, dtype=f32),
            shaped(rows, 768),
            shaped(3, 768, dtype=f32),
        ),
        [position, mine, come, hidden, table, keep, cotangent],
    )
    grad_blocks = share(grad_branch)
    grad_pre, near, far, grad_b_quarter = kernel_call(
        back_kernel,
        "back",
        (
            shaped(4 * rows, 768),
            shaped(2, rows, 768),
            shaped(2, rows, 768),
            shaped(1, 768, dtype=f32),
        ),
        [position, *grad_blocks, slope, w_up, w_down],
    )
    near_feed, far_feed = kernel_call(
        weight_kernel,
        "grad_feed",
        (shaped(4, 192, 768), shaped(4, 192, 768)),
        [position, activated, grad_pre, *hidden_blocks, *grad_blocks],
        [pltpu.VMEM((768, 768), jnp.bfloat16)] * 2,
    )
    come_feed = swap_y(far_feed)
    mine, come = collect(near, far)
    outs = kernel_call(
        attend_back_kernel,
        "attend_back",
        tuple(shaped(2, 4, 48, 768) for _ in range(8))
        + (
            shaped(rows, 768, dtype=f32),
            shaped(rows, 2304),
            shaped(5, 768, dtype=f32),
        ),
        [position, mine, come, grad_second, normed_one, inverse_one, table]
        + [context, proj, weights, w_out, tokens],
        [pltpu.VMEM((768, 3072), jnp.bfloat16)],
        behind=(far_feed,),
    )
    parts_attn = outs[:8]
    grad_first, grad_proj, small_attn = outs[8:]
    last_feed = plus(near_feed, come_feed)
    far, near = sum_parts(parts_attn, swap_parts(parts_attn))
    sums = jnp.concatenate(
        [
            small_attn,
            jnp.where(jnp.arange(REPLICAS)[:, None] == replica, grad_b_quarter, 0.0),
            small_down,
        ]
    )
    sums = sums + swap_z(sums, 1)
    sums = sums + swap_z(sums, 2)
    last_feed, sums = together(last_feed, sums)
    come_attn, across = together(cross_second(far), swap_core(sums))
    zs_feed = send_zs(last_feed)
    onward, stay_attn = sum_plane(near, come_attn)
    sums = sums + across
    come_attn, sums, zs_feed, grad_first = together(
        cross_first(onward), sums, zs_feed, grad_first
    )
    last_attn = sum_last(stay_attn, come_attn)
    zs_attn = send_zs(last_attn)
    reduced_feed = sum_zs(last_feed, zs_feed)
    (grad_tokens,) = kernel_call(
        tokens_kernel,
        "grad_tokens",
        (shaped(rows, 768),),
        [position, grad_first, grad_proj, w_attn],
    )
    sums = sums + swap_x(sums)
    small_total = sums + swap_y(sums)
    far_feed = swap_x(reduced_feed)
    core_feed = swap_core(jnp.stack([reduced_feed, far_feed]))
    d_up, d_down = kernel_call(
        finish_feed_kernel,
        "finish_feed",
        (shaped(96, 3072, dtype=f32), shaped(384, 768, dtype=f32)),
        [position, reduced_feed, far_feed, core_feed],
        [pltpu.VMEM((REPLICAS, 192, 768), jnp.bfloat16)],
    )
    zs_attn, d_up, d_down, grad_tokens, small_total = together(
        zs_attn, d_up, d_down, grad_tokens, small_total
    )
    reduced_attn = sum_zs(last_attn, zs_attn)
    far_attn = swap_x(reduced_attn)
    core_attn = swap_core(jnp.stack([reduced_attn, far_attn]))
    d_qkv, d_out = kernel_call(
        finish_attend_kernel,
        "finish_attend",
        (shaped(96, 2304, dtype=f32), shaped(96, 768, dtype=f32)),
        [position, reduced_attn, far_attn, core_attn],
        [pltpu.VMEM((REPLICAS, 96, 768), jnp.bfloat16)],
    )
    d_qv_bias = lax.dynamic_slice_in_dim(small_total[:2].reshape(-1), shard * 192, 192)
    mine = lax.dynamic_slice_in_dim(small_total[2:], shard * 96, 96, axis=1)
    return (
        layer_out,
        grad_tokens,
        d_qkv,
        d_qv_bias,
        d_out,
        mine[0],
        mine[1],
        mine[2],
        d_up,
        mine[3:7].reshape(-1),
        d_down,
        mine[7],
        mine[8],
        mine[9],
    )


def solution(mesh):
    shape = dict(mesh.shape)
    direct = shape["replica"] == REPLICAS and shape["shard"] == SHARDS
    placed = (
        P(("replica", "shard"), None),
        P(("replica", "shard"), None),
        P("shard", None),
        P("shard"),
        P("shard", None),
        P("shard"),
        P("shard"),
        P("shard"),
        P("shard", None),
        P("shard"),
        P("shard", None),
        P("shard"),
        P("shard"),
        P("shard"),
        P(("replica", "shard"), None),
    )
    return jax.shard_map(
        on_device_direct if direct else on_device_general,
        mesh=mesh,
        in_specs=placed,
        out_specs=(
            P(("replica", "shard"), None),
            P(("replica", "shard"), None),
            P("shard", None),
            P("shard"),
            P("shard", None),
            P("shard"),
            P("shard"),
            P("shard"),
            P("shard", None),
            P("shard"),
            P("shard", None),
            P("shard"),
            P("shard"),
            P("shard"),
        ),
        check_vma=False,
    )
```

```python
from functools import partial

import jax
import jax.numpy as jnp
from jax import lax
from jax.experimental import pallas as pl
from jax.experimental.pallas import tpu as pltpu
from jax.sharding import PartitionSpec as P

HEADS = 12


EPSILON = 1e-05
NEG_FILL = -1e30


def layout(length_row, row_count):
    bounds = jnp.cumsum(length_row)
    places = jnp.arange(row_count, dtype=jnp.int32)
    segment = jnp.sum((places[:, None] >= bounds[None, :]).astype(jnp.int32), axis=1)
    usable = places < bounds[-1]
    segment_id = jnp.where(usable, segment, length_row.shape[0] + places)
    return (segment_id, usable)


def matmul(left_side, right_side):
    return jnp.dot(left_side, right_side, preferred_element_type=jnp.float32)


def matmul_tn(left_side, right_side):
    return lax.dot_general(
        left_side, right_side, (((0,), (0,)), ((), ())), preferred_element_type=jnp.float32
    )


def matmul_nt(left_side, right_side):
    return lax.dot_general(
        left_side, right_side, (((1,), (1,)), ((), ())), preferred_element_type=jnp.float32
    )


def normalize(residual, norm_gain, norm_shift):
    center = residual - jnp.mean(residual, axis=1, keepdims=True)
    inverse = lax.rsqrt(jnp.mean(center * center, axis=1, keepdims=True) + EPSILON)
    normed = center * inverse
    return (normed * norm_gain + norm_shift, normed, inverse)


def normalize_back(grad_out, normed, inverse, norm_gain):
    scaled = grad_out * norm_gain
    grad_in = inverse * (
        scaled
        - jnp.mean(scaled, axis=1, keepdims=True)
        - normed * jnp.mean(scaled * normed, axis=1, keepdims=True)
    )
    return (grad_in, jnp.sum(grad_out * normed, axis=0), jnp.sum(grad_out, axis=0))


def split_heads(tensor):
    return tensor.reshape((tensor.shape[0], HEADS, tensor.shape[1] // HEADS))


def masked_scores(queries, key_rows, same_segment):
    scale_factor = (queries.shape[1] // HEADS) ** (-0.5)
    scores = (
        jnp.einsum(
            "qhd,khd->hqk",
            split_heads(queries),
            split_heads(key_rows),
            preferred_element_type=jnp.float32,
        )
        * scale_factor
    )
    return jnp.where(same_segment[None], scores, NEG_FILL)


def attend(queries, key_rows, values, same_segment):
    masked = masked_scores(queries, key_rows, same_segment)
    highest = jnp.max(masked, axis=2, keepdims=True)
    weights = jnp.exp(masked - highest)
    total = jnp.sum(weights, axis=2, keepdims=True)
    log_total = highest + jnp.log(total)
    attn_probs = (weights / total).astype(jnp.bfloat16)
    context = jnp.einsum(
        "hqk,khd->qhd", attn_probs, split_heads(values), preferred_element_type=jnp.float32
    )
    return (context.reshape(queries.shape).astype(jnp.bfloat16), log_total)


def attend_back(grad_context, queries, key_rows, values, same_segment, log_total):
    scale_factor = (queries.shape[1] // HEADS) ** (-0.5)
    masked = masked_scores(queries, key_rows, same_segment)
    attn_probs = jnp.exp(masked - log_total)
    probs_low = attn_probs.astype(jnp.bfloat16)
    grad_heads = split_heads(grad_context)
    grad_probs = jnp.einsum(
        "qhd,khd->hqk", grad_heads, split_heads(values), preferred_element_type=jnp.float32
    )
    grad_values = jnp.einsum(
        "hqk,qhd->khd", probs_low, grad_heads, preferred_element_type=jnp.float32
    )
    inner = jnp.sum(attn_probs * grad_probs, axis=2, keepdims=True)
    grad_scores = (attn_probs * (grad_probs - inner)).astype(jnp.bfloat16)
    grad_queries = (
        jnp.einsum(
            "hqk,khd->qhd", grad_scores, split_heads(key_rows), preferred_element_type=jnp.float32
        )
        * scale_factor
    )
    grad_keys = (
        jnp.einsum(
            "hqk,qhd->khd", grad_scores, split_heads(queries), preferred_element_type=jnp.float32
        )
        * scale_factor
    )
    shape_flat = queries.shape
    return (
        grad_queries.reshape(shape_flat).astype(jnp.bfloat16),
        grad_keys.reshape(shape_flat).astype(jnp.bfloat16),
        grad_values.reshape(shape_flat).astype(jnp.bfloat16),
    )


AXES = ("replica", "shard")
REPLICAS = 4
SHARDS = 8


def swap_pairs(dx, dcore, dz, dy):
    pairs = []
    for replica in range(REPLICAS):
        for shard in range(SHARDS):
            to_replica = replica ^ (dx * 2 + dcore)
            to_shard = shard ^ (dz * 2 + dy)
            pairs.append((replica * SHARDS + shard, to_replica * SHARDS + to_shard))
    return pairs


def swap_x(value):
    return lax.ppermute(value, AXES, swap_pairs(1, 0, 0, 0))


def swap_core(value):
    return lax.ppermute(value, AXES, swap_pairs(0, 1, 0, 0))


def swap_y(value):
    return lax.ppermute(value, AXES, swap_pairs(0, 0, 0, 1))


def swap_z(value, distance):
    return lax.ppermute(value, AXES, swap_pairs(0, 0, distance, 0))


def together(*trees):
    return lax.optimization_barrier(trees)


def share(block):
    across = swap_x(block)
    return [block, swap_core(block), across, swap_core(across)]


def collect(near, far):
    pair = plus(near, swap_core(far))
    return pair[0], swap_x(pair[1])


def swap_zs(piece):
    return [piece] + [swap_z(piece, distance) for distance in (1, 2, 3)]


def halves_of(pieces):
    half = pieces[0].shape[0] // 2
    return [jnp.stack([entry[at : at + half] for entry in pieces]) for at in (0, half)]


def cross_first(halves):
    return [swap_y(halves[0]), swap_x(halves[1])]


def near_of(halves, come):
    return [jnp.stack(pair) for pair in zip(halves, come)]


def cross_second(near):
    return [swap_x(near[0]), swap_y(near[1])]


def swap_cores(parts):
    return [swap_core(entry) for entry in parts]


def parts_of(near, far, core_near, core_far):
    return [entry for group in zip(near, far, core_near, core_far) for entry in group]


def route(leading, start, rows):
    return [(leading, fixed, core, start, rows) for core in range(2) for fixed in range(2)]


PLAN = route("y", 0, 48) + route("x", 48, 48)


def plus(left_side, right_side):
    return (left_side.astype(jnp.float32) + right_side.astype(jnp.float32)).astype(jnp.bfloat16)


def swap_parts(parts):
    return [swap_core(parts[at]) for at in (3, 7, 2, 6)]


def sum_parts(parts, come):
    far = [plus(parts[1], come[0]), plus(parts[5], come[1])]
    return far, [plus(parts[0], come[2]), plus(parts[4], come[3])]


def sum_plane(near, come):
    onward = [plus(mine[1], other[1]) for mine, other in zip(near, come)]
    return onward, [plus(mine[0], other[0]) for mine, other in zip(near, come)]


def sum_last(stay, come):
    return jnp.concatenate([plus(mine, other) for mine, other in zip(stay, come)], axis=1)


def send_zs(block):
    return [swap_z(block[distance], distance) for distance in (1, 2, 3)]


def sum_zs(block, come):
    total = block[0].astype(jnp.float32)
    for entry in come:
        total = total + entry.astype(jnp.float32)
    return total.astype(jnp.bfloat16)


KERNEL_VMEM = 10 * 2**20
ROOT_HALF = 0.7071067811865476
ROOT_TWO_PI = 0.3989422804014327
VMEM = pl.BlockSpec(memory_space=pltpu.VMEM)
SMEM = pl.BlockSpec(memory_space=pltpu.SMEM)
ROWS_OF = (2, 1, 1, 1, 4, 1, 1, 1)


def kernel_call(kernel, name, out_shapes, inputs, scratch=(), scalars=1, behind=()):
    count = len(inputs)

    def body(*refs):
        kernel(*refs[:count], *refs[count + len(behind) :])

    return pl.pallas_call(
        body,
        out_shape=tuple(out_shapes),
        in_specs=[SMEM] * scalars
        + [VMEM] * (count - scalars)
        + [pl.BlockSpec(memory_space=pl.ANY)] * len(behind),
        out_specs=(VMEM,) * len(out_shapes),
        scratch_shapes=list(scratch),
        compiler_params=pltpu.CompilerParams(vmem_limit_bytes=KERNEL_VMEM),
        cost_estimate=pl.CostEstimate(flops=2**20, bytes_accessed=2**20, transcendentals=0),
        name=name,
    )(*inputs, *behind)


def places(replica, shard):
    for at, (leading, fixed, core, start, count) in enumerate(PLAN):
        for first in range(2):
            x, y = (first, fixed) if leading == "x" else (fixed, first)
            columns = pl.ds(pl.multiple_of((replica ^ (x * 2 + core)) * 768, 128), 768)
            for z in range(4):
                owner = shard ^ (z * 2 + y)
                rows = pl.ds(pl.multiple_of(owner * 96 + start, 16), count)
                yield at, first, z, rows, columns


def segments(lengths, dim, shape):
    at = lax.broadcasted_iota(jnp.int32, shape, dim)
    bound = jnp.int32(0)
    segment = jnp.zeros(shape, jnp.int32)
    for sequence in range(lengths.shape[1]):
        bound = bound + lengths[0, sequence]
        segment = segment + (at >= bound).astype(jnp.int32)
    return jnp.where(at < bound, segment, lengths.shape[1] + at), at < bound


def head_masks(width):
    lane = lax.broadcasted_iota(jnp.int32, (1, width), 1)
    low = lane < width // 2
    return low, [low.astype(jnp.bfloat16), 1.0 - low.astype(jnp.bfloat16)]


def attend_kernel(position, lengths, tokens, packed, *refs):
    parts, refs = refs[:8], refs[8:]
    whole, w_out, proj, weights, context, hidden, hidden_low, normed_one = refs[:8]
    inverse_one, table, keep = refs[8:]
    for at, first, z, rows, columns in places(position[0], position[1]):
        whole[rows, columns] = parts[at][first, z]
    w_out[...] = whole[:, 2304:]
    pieces = packed[...].astype(jnp.float32)
    row, column = 0, 0
    for count in ROWS_OF:
        for at in range(count):
            if count == 2:
                owners = range(at * 4, at * 4 + 4)
                values = [pieces[owner : owner + 1, 0:192] for owner in owners]
            else:
                start = column + at * 96
                values = [pieces[owner : owner + 1, start : start + 96] for owner in range(SHARDS)]
            table[row : row + 1, :] = jnp.concatenate(values, axis=1)
            row += 1
        column += count * 96
    for step in range(3):
        columns = slice(step * 768, (step + 1) * 768)
        projected = matmul(tokens[...], whole[:, columns])
        if step == 0:
            projected = projected + table[0:1, :]
        if step == 2:
            projected = projected + table[1:2, :]
        proj[:, columns] = projected.astype(jnp.bfloat16)
    count = tokens.shape[0]
    across, usable = segments(lengths, 0, (count, 1))
    along, _ = segments(lengths, 1, (1, count))
    keep[...] = usable.astype(jnp.float32)
    same = across == along
    low, masks = head_masks(128)
    for pair in range(HEADS // 2):
        queries, key_rows, values = (
            proj[:, step * 768 + pair * 128 : step * 768 + (pair + 1) * 128] for step in range(3)
        )
        sums = []
        for which in range(2):
            scores = matmul_nt(queries * masks[which], key_rows) * 0.125
            masked = jnp.where(same, scores, NEG_FILL)
            entries = jnp.exp(masked - jnp.max(masked, axis=1, keepdims=True))
            share_of = entries / jnp.sum(entries, axis=1, keepdims=True)
            weights[pair * 2 + which] = share_of
            sums.append(matmul(share_of.astype(jnp.bfloat16), values))
        context[:, pair * 128 : (pair + 1) * 128] = jnp.where(low, sums[0], sums[1]).astype(
            jnp.bfloat16
        )
    attn_out = matmul(context[...], whole[:, 2304:]) + table[2:3, :]
    result, normed, inverse = normalize(
        tokens[...].astype(jnp.float32) + attn_out, table[3:4, :], table[4:5, :]
    )
    hidden[...] = result
    hidden_low[...] = result.astype(jnp.bfloat16)
    normed_one[...] = normed
    inverse_one[...] = inverse


def column_sum(values):
    return jnp.sum(values.astype(jnp.float32), axis=0, keepdims=True)


def attend_back_kernel(
    position,
    mine,
    come,
    grad_second,
    normed_one,
    inverse_one,
    table,
    context,
    proj,
    weights,
    w_out,
    tokens,
    *refs,
):
    parts, refs = refs[:8], refs[8:]
    grad_first, grad_proj, small, total = refs
    grad_hidden = grad_second[...] + (mine[...].astype(jnp.float32) + come[...].astype(jnp.float32))
    grad_in, grad_gain, grad_shift = normalize_back(
        grad_hidden, normed_one[...], inverse_one[...], table[3:4, :]
    )
    grad_first[...] = grad_in
    grad_attn = grad_in.astype(jnp.bfloat16)
    small[2:3, :] = column_sum(grad_attn)
    small[3:4, :] = grad_gain[None, :]
    small[4:5, :] = grad_shift[None, :]
    total[:, 2304:] = matmul_tn(context[...], grad_attn).astype(jnp.bfloat16)
    grad_context = matmul_nt(grad_attn, w_out[...]).astype(jnp.bfloat16)
    low, masks = head_masks(128)
    for pair in range(HEADS // 2):
        queries, key_rows, values = (
            proj[:, step * 768 + pair * 128 : step * 768 + (pair + 1) * 128] for step in range(3)
        )
        grad_pair = grad_context[:, pair * 128 : (pair + 1) * 128]
        sums = []
        for which in range(2):
            share_of = weights[pair * 2 + which]
            grad_probs = matmul_nt(grad_pair * masks[which], values)
            inner = jnp.sum(share_of * grad_probs, axis=1, keepdims=True)
            grad_scores = (share_of * (grad_probs - inner)).astype(jnp.bfloat16)
            sums.append(
                (
                    matmul(grad_scores, key_rows) * 0.125,
                    matmul_tn(grad_scores, queries) * 0.125,
                    matmul_tn(share_of.astype(jnp.bfloat16), grad_pair),
                )
            )
        for step in range(3):
            grad_proj[:, step * 768 + pair * 128 : step * 768 + (pair + 1) * 128] = jnp.where(
                low, sums[0][step], sums[1][step]
            ).astype(jnp.bfloat16)
    for step in range(3):
        columns = slice(step * 768, (step + 1) * 768)
        total[:, columns] = matmul_tn(tokens[...], grad_proj[:, columns]).astype(jnp.bfloat16)
    small[0:1, :] = column_sum(grad_proj[:, :768])
    small[1:2, :] = column_sum(grad_proj[:, 1536:])
    for at, first, z, rows, columns in places(position[0], position[1]):
        parts[at][first, z] = total[rows, columns]


def tokens_kernel(position, grad_first, grad_proj, whole, grad_tokens):
    grad_tokens[...] = (grad_first[...] + matmul_nt(grad_proj[...], whole[:, :2304])).astype(
        jnp.bfloat16
    )


def blocks_of(near, far, shard):
    for y, part in enumerate((near, far)):
        for z in range(4):
            owner = shard ^ (z * 2 + y)
            yield part, z, pl.ds(pl.multiple_of(owner * 96, 16), 96)


def feed_kernel(
    position, own, from_core, from_x, from_both, table, quarter_near, quarter_far, *outs
):
    w_up, w_down, activated, slope, near, far = outs
    for part, z, rows in blocks_of(quarter_near, quarter_far, position[1]):
        w_up[rows, :] = part[z, :96]
        w_down[rows, :] = part[z, 96:]
    bias = table[pl.ds(5 + position[0], 1), :]
    spots = ((near, 0), (far, 0), (near, 1), (far, 1))
    for step, block in enumerate((own, from_core, from_x, from_both)):
        rows = slice(step * 128, (step + 1) * 128)
        pre_act = matmul(block[...], w_up[...]) + bias
        below = 0.5 * (1.0 + lax.erf(pre_act * ROOT_HALF))
        active = (pre_act * below).astype(jnp.bfloat16)
        activated[rows, :] = active
        slope[rows, :] = below + pre_act * (ROOT_TWO_PI * jnp.exp(-0.5 * pre_act * pre_act))
        out, at = spots[step]
        out[at] = matmul(active, w_down[...]).astype(jnp.bfloat16)


def close_kernel(position, mine, come, hidden, table, keep, cotangent, *outs):
    layer_out, grad_second, grad_branch, small = outs
    gain = table[10:11, :]
    branch = mine[...].astype(jnp.float32) + come[...].astype(jnp.float32) + table[9:10, :]
    output_full, normed, inverse = normalize(hidden[...] + branch, gain, table[11:12, :])
    layer_out[...] = (output_full * keep[...]).astype(jnp.bfloat16)
    grad_out = cotangent[...].astype(jnp.float32) * keep[...]
    grad_in, grad_gain, grad_shift = normalize_back(grad_out, normed, inverse, gain)
    low_grad = grad_in.astype(jnp.bfloat16)
    grad_second[...] = grad_in
    grad_branch[...] = low_grad
    small[0:1, :] = jnp.sum(low_grad.astype(jnp.float32), axis=0, keepdims=True)
    small[1:2, :] = grad_gain[None, :]
    small[2:3, :] = grad_shift[None, :]


def back_kernel(position, own, from_core, from_x, from_both, slope, w_up, w_down, *outs):
    grad_pre, near, far, small = outs
    spots = ((near, 0), (far, 0), (near, 1), (far, 1))
    total = jnp.zeros((1, slope.shape[1]), jnp.float32)
    for step, block in enumerate((own, from_core, from_x, from_both)):
        rows = slice(step * 128, (step + 1) * 128)
        grad = matmul_nt(block[...], w_down[...]) * slope[rows, :]
        low_grad = grad.astype(jnp.bfloat16)
        grad_pre[rows, :] = low_grad
        total = total + jnp.sum(low_grad.astype(jnp.float32), axis=0, keepdims=True)
        out, at = spots[step]
        out[at] = matmul_nt(low_grad, w_up[...]).astype(jnp.bfloat16)
    small[...] = total


def weight_kernel(position, activated, grad_pre, *refs):
    hidden_blocks, grad_blocks, (near, far, up, down) = refs[:4], refs[4:8], refs[8:]
    up[...] = matmul_tn(joined(hidden_blocks), grad_pre[...]).astype(jnp.bfloat16)
    down[...] = matmul_tn(activated[...], joined(grad_blocks)).astype(jnp.bfloat16)
    for part, z, rows in blocks_of(near, far, position[1]):
        part[z, :96] = up[rows, :]
        part[z, 96:] = down[rows, :]


def order(position, mine, across, other, blocks):
    replica = position[0]
    blocks[replica] = mine[...]
    blocks[replica ^ 2] = across[...]
    blocks[replica ^ 1] = other[0]
    blocks[replica ^ 3] = other[1]


def finish_feed_kernel(position, mine, across, other, grad_up, grad_down, blocks):
    order(position, mine, across, other, blocks)
    for quarter in range(REPLICAS):
        grad_down[quarter * 96 : (quarter + 1) * 96, :] = blocks[quarter, 96:].astype(jnp.float32)
    for owner in range(SHARDS):
        grad_up[:, owner * 384 : (owner + 1) * 384] = jnp.concatenate(
            [
                blocks[quarter, :96, owner * 96 : (owner + 1) * 96].astype(jnp.float32)
                for quarter in range(REPLICAS)
            ],
            axis=1,
        )


def finish_attend_kernel(position, mine, across, other, grad_qkv, grad_out, blocks):
    order(position, mine, across, other, blocks)
    for quarter in range(3):
        grad_qkv[:, quarter * 768 : (quarter + 1) * 768] = blocks[quarter].astype(jnp.float32)
    grad_out[...] = blocks[3].astype(jnp.float32)


def joined(refs):
    return jnp.concatenate([entry[...] for entry in refs], axis=0)


def small_gather(vector, z, y):
    block = vector[None]
    other = swap_y(block)
    block = jnp.concatenate([jnp.where(y == 0, block, other), jnp.where(y == 0, other, block)])
    for distance in (1, 2):
        other = swap_z(block, distance)
        low_side = (z & distance) == 0
        block = jnp.concatenate(
            [jnp.where(low_side, block, other), jnp.where(low_side, other, block)]
        )
    return block


def on_device_general(
    tokens,
    lengths,
    qkv_weight,
    qv_bias,
    out_weight,
    out_bias,
    first_gain,
    first_shift,
    up_weight,
    up_bias,
    down_weight,
    down_bias,
    second_gain,
    second_shift,
    cotangent,
):
    model_width = tokens.shape[1]
    segment_id, usable = layout(lengths[0], tokens.shape[0])
    same_segment = segment_id[:, None] == segment_id[None, :]
    keep_rows = usable.astype(jnp.float32)[:, None]
    w_qkv, b_qv, w_out, b_out, gain_one, shift_one = (
        lax.all_gather(qkv_weight, "shard", axis=0, tiled=True),
        lax.all_gather(qv_bias, "shard", axis=0, tiled=True),
        lax.all_gather(out_weight, "shard", axis=0, tiled=True),
        lax.all_gather(out_bias, "shard", axis=0, tiled=True),
        lax.all_gather(first_gain, "shard", axis=0, tiled=True),
        lax.all_gather(first_shift, "shard", axis=0, tiled=True),
    )
    projected = matmul(tokens, w_qkv)
    bias_full = b_qv.astype(jnp.float32)
    queries = (projected[:, :model_width] + bias_full[:model_width]).astype(jnp.bfloat16)
    key_rows = projected[:, model_width : 2 * model_width].astype(jnp.bfloat16)
    values = (projected[:, 2 * model_width :] + bias_full[model_width:]).astype(jnp.bfloat16)
    context, log_total = attend(queries, key_rows, values, same_segment)
    attn_out = matmul(context, w_out) + b_out.astype(jnp.float32)
    gain_first = gain_one.astype(jnp.float32)
    hidden, normed_one, inverse_one = normalize(
        tokens.astype(jnp.float32) + attn_out, gain_first, shift_one.astype(jnp.float32)
    )
    hidden_low = hidden.astype(jnp.bfloat16)
    w_up, b_up, w_down, b_down, gain_two, shift_two = (
        lax.all_gather(up_weight, "shard", axis=0, tiled=True),
        lax.all_gather(up_bias, "shard", axis=0, tiled=True),
        lax.all_gather(down_weight, "shard", axis=0, tiled=True),
        lax.all_gather(down_bias, "shard", axis=0, tiled=True),
        lax.all_gather(second_gain, "shard", axis=0, tiled=True),
        lax.all_gather(second_shift, "shard", axis=0, tiled=True),
    )
    pre_act = matmul(hidden_low, w_up) + b_up.astype(jnp.float32)
    activated = jax.nn.gelu(pre_act, approximate=False).astype(jnp.bfloat16)
    branch = matmul(activated, w_down) + b_down.astype(jnp.float32)
    gain_second = gain_two.astype(jnp.float32)
    output_full, normed_two, inverse_two = normalize(
        hidden + branch, gain_second, shift_two.astype(jnp.float32)
    )
    layer_out = (output_full * keep_rows).astype(jnp.bfloat16)
    grad_out = cotangent.astype(jnp.float32) * keep_rows
    grad_second, grad_gain_two, grad_shift_two = normalize_back(
        grad_out, normed_two, inverse_two, gain_second
    )
    back_up, back_down = (w_up, w_down)
    grad_branch = grad_second.astype(jnp.bfloat16)
    grad_w_down = matmul_tn(activated, grad_branch)
    grad_b_down = jnp.sum(grad_branch.astype(jnp.float32), axis=0)
    grad_act = matmul_nt(grad_branch, back_down)
    gelu_value, gelu_pull = jax.vjp(partial(jax.nn.gelu, approximate=False), pre_act)
    grad_pre = gelu_pull(grad_act)[0].astype(jnp.bfloat16)
    grad_w_up = matmul_tn(hidden_low, grad_pre)
    grad_b_up = jnp.sum(grad_pre.astype(jnp.float32), axis=0)
    grad_hidden = grad_second + matmul_nt(grad_pre, back_up)
    ffn_shares = (
        lax.psum_scatter(
            grad_w_up.astype(jnp.bfloat16), "shard", scatter_dimension=0, tiled=True
        ).astype(jnp.float32),
        lax.psum_scatter(
            grad_b_up.astype(jnp.bfloat16), "shard", scatter_dimension=0, tiled=True
        ).astype(jnp.float32),
        lax.psum_scatter(
            grad_w_down.astype(jnp.bfloat16), "shard", scatter_dimension=0, tiled=True
        ).astype(jnp.float32),
        lax.psum_scatter(
            grad_b_down.astype(jnp.bfloat16), "shard", scatter_dimension=0, tiled=True
        ).astype(jnp.float32),
        lax.psum_scatter(
            grad_gain_two.astype(jnp.bfloat16), "shard", scatter_dimension=0, tiled=True
        ).astype(jnp.float32),
        lax.psum_scatter(
            grad_shift_two.astype(jnp.bfloat16), "shard", scatter_dimension=0, tiled=True
        ).astype(jnp.float32),
    )
    grad_first, grad_gain_one, grad_shift_one = normalize_back(
        grad_hidden, normed_one, inverse_one, gain_first
    )
    back_qkv, back_out = (w_qkv, w_out)
    grad_attn = grad_first.astype(jnp.bfloat16)
    grad_w_out = matmul_tn(context, grad_attn)
    grad_b_out = jnp.sum(grad_attn.astype(jnp.float32), axis=0)
    grad_context = matmul_nt(grad_attn, back_out).astype(jnp.bfloat16)
    grad_queries, grad_keys, grad_values = attend_back(
        grad_context, queries, key_rows, values, same_segment, log_total
    )
    grad_proj = jnp.concatenate([grad_queries, grad_keys, grad_values], axis=1)
    grad_w_qkv = matmul_tn(tokens, grad_proj)
    grad_b_qv = jnp.concatenate(
        [
            jnp.sum(grad_queries.astype(jnp.float32), axis=0),
            jnp.sum(grad_values.astype(jnp.float32), axis=0),
        ]
    )
    grad_tokens = (grad_first + matmul_nt(grad_proj, back_qkv)).astype(jnp.bfloat16)
    attn_shares = (
        lax.psum_scatter(
            grad_w_qkv.astype(jnp.bfloat16), "shard", scatter_dimension=0, tiled=True
        ).astype(jnp.float32),
        lax.psum_scatter(
            grad_b_qv.astype(jnp.bfloat16), "shard", scatter_dimension=0, tiled=True
        ).astype(jnp.float32),
        lax.psum_scatter(
            grad_w_out.astype(jnp.bfloat16), "shard", scatter_dimension=0, tiled=True
        ).astype(jnp.float32),
        lax.psum_scatter(
            grad_b_out.astype(jnp.bfloat16), "shard", scatter_dimension=0, tiled=True
        ).astype(jnp.float32),
        lax.psum_scatter(
            grad_gain_one.astype(jnp.bfloat16), "shard", scatter_dimension=0, tiled=True
        ).astype(jnp.float32),
        lax.psum_scatter(
            grad_shift_one.astype(jnp.bfloat16), "shard", scatter_dimension=0, tiled=True
        ).astype(jnp.float32),
    )
    totals = (
        lax.psum(ffn_shares[0].astype(jnp.bfloat16), "replica").astype(jnp.float32),
        lax.psum(ffn_shares[1].astype(jnp.bfloat16), "replica").astype(jnp.float32),
        lax.psum(ffn_shares[2].astype(jnp.bfloat16), "replica").astype(jnp.float32),
        lax.psum(ffn_shares[3].astype(jnp.bfloat16), "replica").astype(jnp.float32),
        lax.psum(ffn_shares[4].astype(jnp.bfloat16), "replica").astype(jnp.float32),
        lax.psum(ffn_shares[5].astype(jnp.bfloat16), "replica").astype(jnp.float32),
        lax.psum(attn_shares[0].astype(jnp.bfloat16), "replica").astype(jnp.float32),
        lax.psum(attn_shares[1].astype(jnp.bfloat16), "replica").astype(jnp.float32),
        lax.psum(attn_shares[2].astype(jnp.bfloat16), "replica").astype(jnp.float32),
        lax.psum(attn_shares[3].astype(jnp.bfloat16), "replica").astype(jnp.float32),
        lax.psum(attn_shares[4].astype(jnp.bfloat16), "replica").astype(jnp.float32),
        lax.psum(attn_shares[5].astype(jnp.bfloat16), "replica").astype(jnp.float32),
    )
    return (
        layer_out,
        grad_tokens,
        totals[6],
        totals[7],
        totals[8],
        totals[9],
        totals[10],
        totals[11],
        totals[0],
        totals[1],
        totals[2],
        totals[3],
        totals[4],
        totals[5],
    )


def on_device_direct(
    tokens,
    lengths,
    qkv_weight,
    qv_bias,
    out_weight,
    out_bias,
    first_gain,
    first_shift,
    up_weight,
    up_bias,
    down_weight,
    down_bias,
    second_gain,
    second_shift,
    cotangent,
):
    rows, model_width = tokens.shape
    replica = lax.axis_index("replica").astype(jnp.int32)
    shard = lax.axis_index("shard").astype(jnp.int32)
    z, y = shard // 2, shard % 2
    position = jnp.stack([replica, shard])
    small = (qv_bias, out_bias, first_gain, first_shift, up_bias, down_bias, second_gain, second_shift)

    def shaped(*shape, dtype=jnp.bfloat16):
        return jax.ShapeDtypeStruct(shape, dtype)

    quarter_attn = jnp.where(
        replica == 3,
        out_weight,
        lax.dynamic_slice_in_dim(qkv_weight, jnp.minimum(replica, 2) * 768, 768, axis=1),
    )
    quarter_up = lax.dynamic_index_in_dim(
        up_weight.reshape(up_weight.shape[0], SHARDS, REPLICAS, -1), replica, 2, False
    ).reshape(-1, 768)
    quarter_down = lax.dynamic_slice_in_dim(down_weight, replica * 96, 96, axis=0)
    z_attn = swap_zs(quarter_attn)
    packed = small_gather(jnp.concatenate(small), z, y)
    quarter_feed = jnp.concatenate([quarter_up, quarter_down])
    z_attn, quarter_feed = together(z_attn, quarter_feed)
    z_feed = swap_zs(quarter_feed)
    half_attn = halves_of(z_attn)
    near_attn = near_of(half_attn, cross_first(half_attn))
    far_attn = cross_second(near_attn)
    far_attn, near_attn, packed = together(far_attn, near_attn, packed)
    core_attn = parts_of(near_attn, far_attn, swap_cores(near_attn), swap_cores(far_attn))
    near_feed = jnp.stack(z_feed)
    far_feed = swap_y(near_feed)
    f32 = jnp.float32
    (
        w_attn,
        w_out,
        proj,
        weights,
        context,
        hidden,
        hidden_low,
        normed_one,
        inverse_one,
        table,
        keep,
    ) = kernel_call(
        attend_kernel,
        "attend",
        (
            shaped(768, 3072),
            shaped(768, 768),
            shaped(rows, 2304),
            shaped(HEADS, rows, rows, dtype=f32),
            shaped(rows, 768),
            shaped(rows, 768, dtype=f32),
            shaped(rows, 768),
            shaped(rows, 768, dtype=f32),
            shaped(rows, 1, dtype=f32),
            shaped(12, 768, dtype=f32),
            shaped(rows, 1, dtype=f32),
        ),
        [position, lengths, tokens, packed] + core_attn,
        scalars=2,
        behind=(near_feed,),
    )
    hidden_blocks = share(hidden_low)
    w_up, w_down, activated, slope, near, far = kernel_call(
        feed_kernel,
        "feed",
        (
            shaped(768, 768),
            shaped(768, 768),
            shaped(4 * rows, 768),
            shaped(4 * rows, 768, dtype=f32),
            shaped(2, rows, 768),
            shaped(2, rows, 768),
        ),
        [position, *hidden_blocks, table, near_feed, far_feed],
    )
    mine, come = collect(near, far)
    layer_out, grad_second, grad_branch, small_down = kernel_call(
        close_kernel,
        "close",
        (
            shaped(rows, 768),
            shaped(rows, 768, dtype=f32),
            shaped(rows, 768),
            shaped(3, 768, dtype=f32),
        ),
        [position, mine, come, hidden, table, keep, cotangent],
    )
    grad_blocks = share(grad_branch)
    grad_pre, near, far, grad_b_quarter = kernel_call(
        back_kernel,
        "back",
        (
            shaped(4 * rows, 768),
            shaped(2, rows, 768),
            shaped(2, rows, 768),
            shaped(1, 768, dtype=f32),
        ),
        [position, *grad_blocks, slope, w_up, w_down],
    )
    near_feed, far_feed = kernel_call(
        weight_kernel,
        "grad_feed",
        (shaped(4, 192, 768), shaped(4, 192, 768)),
        [position, activated, grad_pre, *hidden_blocks, *grad_blocks],
        [pltpu.VMEM((768, 768), jnp.bfloat16)] * 2,
    )
    come_feed = swap_y(far_feed)
    mine, come = collect(near, far)
    outs = kernel_call(
        attend_back_kernel,
        "attend_back",
        tuple(shaped(2, 4, 48, 768) for _ in range(8))
        + (
            shaped(rows, 768, dtype=f32),
            shaped(rows, 2304),
            shaped(5, 768, dtype=f32),
        ),
        [position, mine, come, grad_second, normed_one, inverse_one, table]
        + [context, proj, weights, w_out, tokens],
        [pltpu.VMEM((768, 3072), jnp.bfloat16)],
        behind=(far_feed,),
    )
    parts_attn = outs[:8]
    grad_first, grad_proj, small_attn = outs[8:]
    last_feed = plus(near_feed, come_feed)
    far, near = sum_parts(parts_attn, swap_parts(parts_attn))
    sums = jnp.concatenate(
        [
            small_attn,
            jnp.where(jnp.arange(REPLICAS)[:, None] == replica, grad_b_quarter, 0.0),
            small_down,
        ]
    )
    sums = sums + swap_z(sums, 1)
    sums = sums + swap_z(sums, 2)
    come_attn = cross_second(far)
    zs_feed = send_zs(last_feed)
    onward, stay_attn = sum_plane(near, come_attn)
    come_attn, sums, zs_feed, grad_first = together(
        cross_first(onward), sums, zs_feed, grad_first
    )
    last_attn = sum_last(stay_attn, come_attn)
    zs_attn = send_zs(last_attn)
    reduced_feed = sum_zs(last_feed, zs_feed)
    far_feed = swap_x(reduced_feed)
    (grad_tokens,) = kernel_call(
        tokens_kernel,
        "grad_tokens",
        (shaped(rows, 768),),
        [position, grad_first, grad_proj, w_attn],
    )
    sums = sums + swap_core(sums)
    sums = sums + swap_x(sums)
    small_total = sums + swap_y(sums)
    zs_attn, far_feed, grad_tokens, small_total = together(
        zs_attn, far_feed, grad_tokens, small_total
    )
    core_feed = swap_core(jnp.stack([reduced_feed, far_feed]))
    d_up, d_down = kernel_call(
        finish_feed_kernel,
        "finish_feed",
        (shaped(96, 3072, dtype=f32), shaped(384, 768, dtype=f32)),
        [position, reduced_feed, far_feed, core_feed],
        [pltpu.VMEM((REPLICAS, 192, 768), jnp.bfloat16)],
    )
    reduced_attn = sum_zs(last_attn, zs_attn)
    far_attn = swap_x(reduced_attn)
    core_attn = swap_core(jnp.stack([reduced_attn, far_attn]))
    d_qkv, d_out = kernel_call(
        finish_attend_kernel,
        "finish_attend",
        (shaped(96, 2304, dtype=f32), shaped(96, 768, dtype=f32)),
        [position, reduced_attn, far_attn, core_attn],
        [pltpu.VMEM((REPLICAS, 96, 768), jnp.bfloat16)],
    )
    d_qv_bias = lax.dynamic_slice_in_dim(small_total[:2].reshape(-1), shard * 192, 192)
    mine = lax.dynamic_slice_in_dim(small_total[2:], shard * 96, 96, axis=1)
    return (
        layer_out,
        grad_tokens,
        d_qkv,
        d_qv_bias,
        d_out,
        mine[0],
        mine[1],
        mine[2],
        d_up,
        mine[3:7].reshape(-1),
        d_down,
        mine[7],
        mine[8],
        mine[9],
    )


def solution(mesh):
    shape = dict(mesh.shape)
    direct = shape["replica"] == REPLICAS and shape["shard"] == SHARDS
    placed = (
        P(("replica", "shard"), None),
        P(("replica", "shard"), None),
        P("shard", None),
        P("shard"),
        P("shard", None),
        P("shard"),
        P("shard"),
        P("shard"),
        P("shard", None),
        P("shard"),
        P("shard", None),
        P("shard"),
        P("shard"),
        P("shard"),
        P(("replica", "shard"), None),
    )
    return jax.shard_map(
        on_device_direct if direct else on_device_general,
        mesh=mesh,
        in_specs=placed,
        out_specs=(
            P(("replica", "shard"), None),
            P(("replica", "shard"), None),
            P("shard", None),
            P("shard"),
            P("shard", None),
            P("shard"),
            P("shard"),
            P("shard"),
            P("shard", None),
            P("shard"),
            P("shard", None),
            P("shard"),
            P("shard"),
            P("shard"),
        ),
        check_vma=False,
    )
```

```python
from functools import partial

import jax
import jax.numpy as jnp
from jax import lax
from jax.experimental import pallas as pl
from jax.experimental.pallas import tpu as pltpu
from jax.sharding import PartitionSpec as P

HEADS = 12


EPSILON = 1e-05
NEG_FILL = -1e30


def layout(length_row, row_count):
    bounds = jnp.cumsum(length_row)
    places = jnp.arange(row_count, dtype=jnp.int32)
    segment = jnp.sum((places[:, None] >= bounds[None, :]).astype(jnp.int32), axis=1)
    usable = places < bounds[-1]
    segment_id = jnp.where(usable, segment, length_row.shape[0] + places)
    return (segment_id, usable)


def matmul(left_side, right_side):
    return jnp.dot(left_side, right_side, preferred_element_type=jnp.float32)


def matmul_tn(left_side, right_side):
    return lax.dot_general(
        left_side, right_side, (((0,), (0,)), ((), ())), preferred_element_type=jnp.float32
    )


def matmul_nt(left_side, right_side):
    return lax.dot_general(
        left_side, right_side, (((1,), (1,)), ((), ())), preferred_element_type=jnp.float32
    )


def normalize(residual, norm_gain, norm_shift):
    center = residual - jnp.mean(residual, axis=1, keepdims=True)
    inverse = lax.rsqrt(jnp.mean(center * center, axis=1, keepdims=True) + EPSILON)
    normed = center * inverse
    return (normed * norm_gain + norm_shift, normed, inverse)


def normalize_back(grad_out, normed, inverse, norm_gain):
    scaled = grad_out * norm_gain
    grad_in = inverse * (
        scaled
        - jnp.mean(scaled, axis=1, keepdims=True)
        - normed * jnp.mean(scaled * normed, axis=1, keepdims=True)
    )
    return (grad_in, jnp.sum(grad_out * normed, axis=0), jnp.sum(grad_out, axis=0))


def split_heads(tensor):
    return tensor.reshape((tensor.shape[0], HEADS, tensor.shape[1] // HEADS))


def masked_scores(queries, key_rows, same_segment):
    scale_factor = (queries.shape[1] // HEADS) ** (-0.5)
    scores = (
        jnp.einsum(
            "qhd,khd->hqk",
            split_heads(queries),
            split_heads(key_rows),
            preferred_element_type=jnp.float32,
        )
        * scale_factor
    )
    return jnp.where(same_segment[None], scores, NEG_FILL)


def attend(queries, key_rows, values, same_segment):
    masked = masked_scores(queries, key_rows, same_segment)
    highest = jnp.max(masked, axis=2, keepdims=True)
    weights = jnp.exp(masked - highest)
    total = jnp.sum(weights, axis=2, keepdims=True)
    log_total = highest + jnp.log(total)
    attn_probs = (weights / total).astype(jnp.bfloat16)
    context = jnp.einsum(
        "hqk,khd->qhd", attn_probs, split_heads(values), preferred_element_type=jnp.float32
    )
    return (context.reshape(queries.shape).astype(jnp.bfloat16), log_total)


def attend_back(grad_context, queries, key_rows, values, same_segment, log_total):
    scale_factor = (queries.shape[1] // HEADS) ** (-0.5)
    masked = masked_scores(queries, key_rows, same_segment)
    attn_probs = jnp.exp(masked - log_total)
    probs_low = attn_probs.astype(jnp.bfloat16)
    grad_heads = split_heads(grad_context)
    grad_probs = jnp.einsum(
        "qhd,khd->hqk", grad_heads, split_heads(values), preferred_element_type=jnp.float32
    )
    grad_values = jnp.einsum(
        "hqk,qhd->khd", probs_low, grad_heads, preferred_element_type=jnp.float32
    )
    inner = jnp.sum(attn_probs * grad_probs, axis=2, keepdims=True)
    grad_scores = (attn_probs * (grad_probs - inner)).astype(jnp.bfloat16)
    grad_queries = (
        jnp.einsum(
            "hqk,khd->qhd", grad_scores, split_heads(key_rows), preferred_element_type=jnp.float32
        )
        * scale_factor
    )
    grad_keys = (
        jnp.einsum(
            "hqk,qhd->khd", grad_scores, split_heads(queries), preferred_element_type=jnp.float32
        )
        * scale_factor
    )
    shape_flat = queries.shape
    return (
        grad_queries.reshape(shape_flat).astype(jnp.bfloat16),
        grad_keys.reshape(shape_flat).astype(jnp.bfloat16),
        grad_values.reshape(shape_flat).astype(jnp.bfloat16),
    )


AXES = ("replica", "shard")
REPLICAS = 4
SHARDS = 8


def swap_pairs(dx, dcore, dz, dy):
    pairs = []
    for replica in range(REPLICAS):
        for shard in range(SHARDS):
            to_replica = replica ^ (dx * 2 + dcore)
            to_shard = shard ^ (dz * 2 + dy)
            pairs.append((replica * SHARDS + shard, to_replica * SHARDS + to_shard))
    return pairs


def swap_x(value):
    return lax.ppermute(value, AXES, swap_pairs(1, 0, 0, 0))


def swap_core(value):
    return lax.ppermute(value, AXES, swap_pairs(0, 1, 0, 0))


def swap_y(value):
    return lax.ppermute(value, AXES, swap_pairs(0, 0, 0, 1))


def swap_z(value, distance):
    return lax.ppermute(value, AXES, swap_pairs(0, 0, distance, 0))


def together(*trees):
    return lax.optimization_barrier(trees)


def share(block):
    across = swap_x(block)
    return [block, swap_core(block), across, swap_core(across)]


def collect(near, far):
    pair = plus(near, swap_core(far))
    return pair[0], swap_x(pair[1])


def swap_zs(piece):
    return [piece] + [swap_z(piece, distance) for distance in (1, 2, 3)]


def halves_of(pieces):
    half = pieces[0].shape[0] // 2
    return [jnp.stack([entry[at : at + half] for entry in pieces]) for at in (0, half)]


def cross_first(halves):
    return [swap_y(halves[0]), swap_x(halves[1])]


def near_of(halves, come):
    return [jnp.stack(pair) for pair in zip(halves, come)]


def cross_second(near):
    return [swap_x(near[0]), swap_y(near[1])]


def swap_cores(parts):
    return [swap_core(entry) for entry in parts]


def parts_of(near, far, core_near, core_far):
    return [entry for group in zip(near, far, core_near, core_far) for entry in group]


def route(leading, start, rows):
    return [(leading, fixed, core, start, rows) for core in range(2) for fixed in range(2)]


PLAN = route("y", 0, 48) + route("x", 48, 48)


def plus(left_side, right_side):
    return (left_side.astype(jnp.float32) + right_side.astype(jnp.float32)).astype(jnp.bfloat16)


def swap_parts(parts):
    return [swap_core(parts[at]) for at in (3, 7, 2, 6)]


def sum_parts(parts, come):
    far = [plus(parts[1], come[0]), plus(parts[5], come[1])]
    return far, [plus(parts[0], come[2]), plus(parts[4], come[3])]


def sum_plane(near, come):
    onward = [plus(mine[1], other[1]) for mine, other in zip(near, come)]
    return onward, [plus(mine[0], other[0]) for mine, other in zip(near, come)]


def sum_last(stay, come):
    return jnp.concatenate([plus(mine, other) for mine, other in zip(stay, come)], axis=1)


def send_zs(block):
    return [swap_z(block[distance], distance) for distance in (1, 2, 3)]


def sum_zs(block, come):
    total = block[0].astype(jnp.float32)
    for entry in come:
        total = total + entry.astype(jnp.float32)
    return total.astype(jnp.bfloat16)


KERNEL_VMEM = 10 * 2**20
ROOT_HALF = 0.7071067811865476
ROOT_TWO_PI = 0.3989422804014327
VMEM = pl.BlockSpec(memory_space=pltpu.VMEM)
SMEM = pl.BlockSpec(memory_space=pltpu.SMEM)
ROWS_OF = (2, 1, 1, 1, 4, 1, 1, 1)


def kernel_call(kernel, name, out_shapes, inputs, scratch=(), scalars=1, behind=()):
    count = len(inputs)

    def body(*refs):
        kernel(*refs[:count], *refs[count + len(behind) :])

    return pl.pallas_call(
        body,
        out_shape=tuple(out_shapes),
        in_specs=[SMEM] * scalars
        + [VMEM] * (count - scalars)
        + [pl.BlockSpec(memory_space=pl.ANY)] * len(behind),
        out_specs=(VMEM,) * len(out_shapes),
        scratch_shapes=list(scratch),
        compiler_params=pltpu.CompilerParams(vmem_limit_bytes=KERNEL_VMEM),
        cost_estimate=pl.CostEstimate(flops=2**20, bytes_accessed=2**20, transcendentals=0),
        name=name,
    )(*inputs, *behind)


def places(replica, shard):
    for at, (leading, fixed, core, start, count) in enumerate(PLAN):
        for first in range(2):
            x, y = (first, fixed) if leading == "x" else (fixed, first)
            columns = pl.ds(pl.multiple_of((replica ^ (x * 2 + core)) * 768, 128), 768)
            for z in range(4):
                owner = shard ^ (z * 2 + y)
                rows = pl.ds(pl.multiple_of(owner * 96 + start, 16), count)
                yield at, first, z, rows, columns


def segments(lengths, dim, shape):
    at = lax.broadcasted_iota(jnp.int32, shape, dim)
    bound = jnp.int32(0)
    segment = jnp.zeros(shape, jnp.int32)
    for sequence in range(lengths.shape[1]):
        bound = bound + lengths[0, sequence]
        segment = segment + (at >= bound).astype(jnp.int32)
    return jnp.where(at < bound, segment, lengths.shape[1] + at), at < bound


def head_masks(width):
    lane = lax.broadcasted_iota(jnp.int32, (1, width), 1)
    low = lane < width // 2
    return low, [low.astype(jnp.bfloat16), 1.0 - low.astype(jnp.bfloat16)]


def attend_kernel(position, lengths, tokens, packed, *refs):
    parts, refs = refs[:8], refs[8:]
    whole, w_out, proj, weights, context, hidden, hidden_low, normed_one = refs[:8]
    inverse_one, table, keep = refs[8:]
    for at, first, z, rows, columns in places(position[0], position[1]):
        whole[rows, columns] = parts[at][first, z]
    w_out[...] = whole[:, 2304:]
    pieces = packed[...].astype(jnp.float32)
    row, column = 0, 0
    for count in ROWS_OF:
        for at in range(count):
            if count == 2:
                owners = range(at * 4, at * 4 + 4)
                values = [pieces[owner : owner + 1, 0:192] for owner in owners]
            else:
                start = column + at * 96
                values = [pieces[owner : owner + 1, start : start + 96] for owner in range(SHARDS)]
            table[row : row + 1, :] = jnp.concatenate(values, axis=1)
            row += 1
        column += count * 96
    for step in range(3):
        columns = slice(step * 768, (step + 1) * 768)
        projected = matmul(tokens[...], whole[:, columns])
        if step == 0:
            projected = projected + table[0:1, :]
        if step == 2:
            projected = projected + table[1:2, :]
        proj[:, columns] = projected.astype(jnp.bfloat16)
    count = tokens.shape[0]
    across, usable = segments(lengths, 0, (count, 1))
    along, _ = segments(lengths, 1, (1, count))
    keep[...] = usable.astype(jnp.float32)
    same = across == along
    low, masks = head_masks(128)
    for pair in range(HEADS // 2):
        queries, key_rows, values = (
            proj[:, step * 768 + pair * 128 : step * 768 + (pair + 1) * 128] for step in range(3)
        )
        sums = []
        for which in range(2):
            scores = matmul_nt(queries * masks[which], key_rows) * 0.125
            masked = jnp.where(same, scores, NEG_FILL)
            entries = jnp.exp(masked - jnp.max(masked, axis=1, keepdims=True))
            share_of = entries / jnp.sum(entries, axis=1, keepdims=True)
            weights[pair * 2 + which] = share_of
            sums.append(matmul(share_of.astype(jnp.bfloat16), values))
        context[:, pair * 128 : (pair + 1) * 128] = jnp.where(low, sums[0], sums[1]).astype(
            jnp.bfloat16
        )
    attn_out = matmul(context[...], whole[:, 2304:]) + table[2:3, :]
    result, normed, inverse = normalize(
        tokens[...].astype(jnp.float32) + attn_out, table[3:4, :], table[4:5, :]
    )
    hidden[...] = result
    hidden_low[...] = result.astype(jnp.bfloat16)
    normed_one[...] = normed
    inverse_one[...] = inverse


def column_sum(values):
    return jnp.sum(values.astype(jnp.float32), axis=0, keepdims=True)


def attend_back_kernel(
    position,
    mine,
    come,
    grad_second,
    normed_one,
    inverse_one,
    table,
    context,
    proj,
    weights,
    w_out,
    tokens,
    *refs,
):
    parts, refs = refs[:8], refs[8:]
    grad_first, grad_proj, small, total = refs
    grad_hidden = grad_second[...] + (mine[...].astype(jnp.float32) + come[...].astype(jnp.float32))
    grad_in, grad_gain, grad_shift = normalize_back(
        grad_hidden, normed_one[...], inverse_one[...], table[3:4, :]
    )
    grad_first[...] = grad_in
    grad_attn = grad_in.astype(jnp.bfloat16)
    small[2:3, :] = column_sum(grad_attn)
    small[3:4, :] = grad_gain[None, :]
    small[4:5, :] = grad_shift[None, :]
    total[:, 2304:] = matmul_tn(context[...], grad_attn).astype(jnp.bfloat16)
    grad_context = matmul_nt(grad_attn, w_out[...]).astype(jnp.bfloat16)
    low, masks = head_masks(128)
    for pair in range(HEADS // 2):
        queries, key_rows, values = (
            proj[:, step * 768 + pair * 128 : step * 768 + (pair + 1) * 128] for step in range(3)
        )
        grad_pair = grad_context[:, pair * 128 : (pair + 1) * 128]
        sums = []
        for which in range(2):
            share_of = weights[pair * 2 + which]
            grad_probs = matmul_nt(grad_pair * masks[which], values)
            inner = jnp.sum(share_of * grad_probs, axis=1, keepdims=True)
            grad_scores = (share_of * (grad_probs - inner)).astype(jnp.bfloat16)
            sums.append(
                (
                    matmul(grad_scores, key_rows) * 0.125,
                    matmul_tn(grad_scores, queries) * 0.125,
                    matmul_tn(share_of.astype(jnp.bfloat16), grad_pair),
                )
            )
        for step in range(3):
            grad_proj[:, step * 768 + pair * 128 : step * 768 + (pair + 1) * 128] = jnp.where(
                low, sums[0][step], sums[1][step]
            ).astype(jnp.bfloat16)
    for step in range(3):
        columns = slice(step * 768, (step + 1) * 768)
        total[:, columns] = matmul_tn(tokens[...], grad_proj[:, columns]).astype(jnp.bfloat16)
    small[0:1, :] = column_sum(grad_proj[:, :768])
    small[1:2, :] = column_sum(grad_proj[:, 1536:])
    for at, first, z, rows, columns in places(position[0], position[1]):
        parts[at][first, z] = total[rows, columns]


def tokens_kernel(position, grad_first, grad_proj, whole, grad_tokens):
    grad_tokens[...] = (grad_first[...] + matmul_nt(grad_proj[...], whole[:, :2304])).astype(
        jnp.bfloat16
    )


def blocks_of(near, far, shard):
    for y, part in enumerate((near, far)):
        for z in range(4):
            owner = shard ^ (z * 2 + y)
            yield part, z, pl.ds(pl.multiple_of(owner * 96, 16), 96)


def feed_kernel(
    position, own, from_core, from_x, from_both, table, quarter_near, quarter_far, *outs
):
    w_up, w_down, activated, slope, near, far = outs
    for part, z, rows in blocks_of(quarter_near, quarter_far, position[1]):
        w_up[rows, :] = part[z, :96]
        w_down[rows, :] = part[z, 96:]
    bias = table[pl.ds(5 + position[0], 1), :]
    spots = ((near, 0), (far, 0), (near, 1), (far, 1))
    for step, block in enumerate((own, from_core, from_x, from_both)):
        rows = slice(step * 128, (step + 1) * 128)
        pre_act = matmul(block[...], w_up[...]) + bias
        below = 0.5 * (1.0 + lax.erf(pre_act * ROOT_HALF))
        active = (pre_act * below).astype(jnp.bfloat16)
        activated[rows, :] = active
        slope[rows, :] = below + pre_act * (ROOT_TWO_PI * jnp.exp(-0.5 * pre_act * pre_act))
        out, at = spots[step]
        out[at] = matmul(active, w_down[...]).astype(jnp.bfloat16)


def close_kernel(position, mine, come, hidden, table, keep, cotangent, *outs):
    layer_out, grad_second, grad_branch, small = outs
    gain = table[10:11, :]
    branch = mine[...].astype(jnp.float32) + come[...].astype(jnp.float32) + table[9:10, :]
    output_full, normed, inverse = normalize(hidden[...] + branch, gain, table[11:12, :])
    layer_out[...] = (output_full * keep[...]).astype(jnp.bfloat16)
    grad_out = cotangent[...].astype(jnp.float32) * keep[...]
    grad_in, grad_gain, grad_shift = normalize_back(grad_out, normed, inverse, gain)
    low_grad = grad_in.astype(jnp.bfloat16)
    grad_second[...] = grad_in
    grad_branch[...] = low_grad
    small[0:1, :] = jnp.sum(low_grad.astype(jnp.float32), axis=0, keepdims=True)
    small[1:2, :] = grad_gain[None, :]
    small[2:3, :] = grad_shift[None, :]


def back_kernel(position, own, from_core, from_x, from_both, slope, w_up, w_down, *outs):
    grad_pre, near, far, small = outs
    spots = ((near, 0), (far, 0), (near, 1), (far, 1))
    total = jnp.zeros((1, slope.shape[1]), jnp.float32)
    for step, block in enumerate((own, from_core, from_x, from_both)):
        rows = slice(step * 128, (step + 1) * 128)
        grad = matmul_nt(block[...], w_down[...]) * slope[rows, :]
        low_grad = grad.astype(jnp.bfloat16)
        grad_pre[rows, :] = low_grad
        total = total + jnp.sum(low_grad.astype(jnp.float32), axis=0, keepdims=True)
        out, at = spots[step]
        out[at] = matmul_nt(low_grad, w_up[...]).astype(jnp.bfloat16)
    small[...] = total


def weight_kernel(position, activated, grad_pre, *refs):
    hidden_blocks, grad_blocks, (near, far, up, down) = refs[:4], refs[4:8], refs[8:]
    up[...] = matmul_tn(joined(hidden_blocks), grad_pre[...]).astype(jnp.bfloat16)
    down[...] = matmul_tn(activated[...], joined(grad_blocks)).astype(jnp.bfloat16)
    for part, z, rows in blocks_of(near, far, position[1]):
        part[z, :96] = up[rows, :]
        part[z, 96:] = down[rows, :]


def order(position, mine, across, other, blocks):
    replica = position[0]
    blocks[replica] = mine[...]
    blocks[replica ^ 2] = across[...]
    blocks[replica ^ 1] = other[0]
    blocks[replica ^ 3] = other[1]


def finish_feed_kernel(position, mine, across, other, grad_up, grad_down, blocks):
    order(position, mine, across, other, blocks)
    for quarter in range(REPLICAS):
        grad_down[quarter * 96 : (quarter + 1) * 96, :] = blocks[quarter, 96:].astype(jnp.float32)
    for owner in range(SHARDS):
        grad_up[:, owner * 384 : (owner + 1) * 384] = jnp.concatenate(
            [
                blocks[quarter, :96, owner * 96 : (owner + 1) * 96].astype(jnp.float32)
                for quarter in range(REPLICAS)
            ],
            axis=1,
        )


def finish_attend_kernel(position, mine, across, other, grad_qkv, grad_out, blocks):
    order(position, mine, across, other, blocks)
    for quarter in range(3):
        grad_qkv[:, quarter * 768 : (quarter + 1) * 768] = blocks[quarter].astype(jnp.float32)
    grad_out[...] = blocks[3].astype(jnp.float32)


def joined(refs):
    return jnp.concatenate([entry[...] for entry in refs], axis=0)


def small_gather(vector, z, y):
    block = vector[None]
    other = swap_y(block)
    block = jnp.concatenate([jnp.where(y == 0, block, other), jnp.where(y == 0, other, block)])
    for distance in (1, 2):
        other = swap_z(block, distance)
        low_side = (z & distance) == 0
        block = jnp.concatenate(
            [jnp.where(low_side, block, other), jnp.where(low_side, other, block)]
        )
    return block


def on_device_general(
    tokens,
    lengths,
    qkv_weight,
    qv_bias,
    out_weight,
    out_bias,
    first_gain,
    first_shift,
    up_weight,
    up_bias,
    down_weight,
    down_bias,
    second_gain,
    second_shift,
    cotangent,
):
    model_width = tokens.shape[1]
    segment_id, usable = layout(lengths[0], tokens.shape[0])
    same_segment = segment_id[:, None] == segment_id[None, :]
    keep_rows = usable.astype(jnp.float32)[:, None]
    w_qkv, b_qv, w_out, b_out, gain_one, shift_one = (
        lax.all_gather(qkv_weight, "shard", axis=0, tiled=True),
        lax.all_gather(qv_bias, "shard", axis=0, tiled=True),
        lax.all_gather(out_weight, "shard", axis=0, tiled=True),
        lax.all_gather(out_bias, "shard", axis=0, tiled=True),
        lax.all_gather(first_gain, "shard", axis=0, tiled=True),
        lax.all_gather(first_shift, "shard", axis=0, tiled=True),
    )
    projected = matmul(tokens, w_qkv)
    bias_full = b_qv.astype(jnp.float32)
    queries = (projected[:, :model_width] + bias_full[:model_width]).astype(jnp.bfloat16)
    key_rows = projected[:, model_width : 2 * model_width].astype(jnp.bfloat16)
    values = (projected[:, 2 * model_width :] + bias_full[model_width:]).astype(jnp.bfloat16)
    context, log_total = attend(queries, key_rows, values, same_segment)
    attn_out = matmul(context, w_out) + b_out.astype(jnp.float32)
    gain_first = gain_one.astype(jnp.float32)
    hidden, normed_one, inverse_one = normalize(
        tokens.astype(jnp.float32) + attn_out, gain_first, shift_one.astype(jnp.float32)
    )
    hidden_low = hidden.astype(jnp.bfloat16)
    w_up, b_up, w_down, b_down, gain_two, shift_two = (
        lax.all_gather(up_weight, "shard", axis=0, tiled=True),
        lax.all_gather(up_bias, "shard", axis=0, tiled=True),
        lax.all_gather(down_weight, "shard", axis=0, tiled=True),
        lax.all_gather(down_bias, "shard", axis=0, tiled=True),
        lax.all_gather(second_gain, "shard", axis=0, tiled=True),
        lax.all_gather(second_shift, "shard", axis=0, tiled=True),
    )
    pre_act = matmul(hidden_low, w_up) + b_up.astype(jnp.float32)
    activated = jax.nn.gelu(pre_act, approximate=False).astype(jnp.bfloat16)
    branch = matmul(activated, w_down) + b_down.astype(jnp.float32)
    gain_second = gain_two.astype(jnp.float32)
    output_full, normed_two, inverse_two = normalize(
        hidden + branch, gain_second, shift_two.astype(jnp.float32)
    )
    layer_out = (output_full * keep_rows).astype(jnp.bfloat16)
    grad_out = cotangent.astype(jnp.float32) * keep_rows
    grad_second, grad_gain_two, grad_shift_two = normalize_back(
        grad_out, normed_two, inverse_two, gain_second
    )
    back_up, back_down = (w_up, w_down)
    grad_branch = grad_second.astype(jnp.bfloat16)
    grad_w_down = matmul_tn(activated, grad_branch)
    grad_b_down = jnp.sum(grad_branch.astype(jnp.float32), axis=0)
    grad_act = matmul_nt(grad_branch, back_down)
    gelu_value, gelu_pull = jax.vjp(partial(jax.nn.gelu, approximate=False), pre_act)
    grad_pre = gelu_pull(grad_act)[0].astype(jnp.bfloat16)
    grad_w_up = matmul_tn(hidden_low, grad_pre)
    grad_b_up = jnp.sum(grad_pre.astype(jnp.float32), axis=0)
    grad_hidden = grad_second + matmul_nt(grad_pre, back_up)
    ffn_shares = (
        lax.psum_scatter(
            grad_w_up.astype(jnp.bfloat16), "shard", scatter_dimension=0, tiled=True
        ).astype(jnp.float32),
        lax.psum_scatter(
            grad_b_up.astype(jnp.bfloat16), "shard", scatter_dimension=0, tiled=True
        ).astype(jnp.float32),
        lax.psum_scatter(
            grad_w_down.astype(jnp.bfloat16), "shard", scatter_dimension=0, tiled=True
        ).astype(jnp.float32),
        lax.psum_scatter(
            grad_b_down.astype(jnp.bfloat16), "shard", scatter_dimension=0, tiled=True
        ).astype(jnp.float32),
        lax.psum_scatter(
            grad_gain_two.astype(jnp.bfloat16), "shard", scatter_dimension=0, tiled=True
        ).astype(jnp.float32),
        lax.psum_scatter(
            grad_shift_two.astype(jnp.bfloat16), "shard", scatter_dimension=0, tiled=True
        ).astype(jnp.float32),
    )
    grad_first, grad_gain_one, grad_shift_one = normalize_back(
        grad_hidden, normed_one, inverse_one, gain_first
    )
    back_qkv, back_out = (w_qkv, w_out)
    grad_attn = grad_first.astype(jnp.bfloat16)
    grad_w_out = matmul_tn(context, grad_attn)
    grad_b_out = jnp.sum(grad_attn.astype(jnp.float32), axis=0)
    grad_context = matmul_nt(grad_attn, back_out).astype(jnp.bfloat16)
    grad_queries, grad_keys, grad_values = attend_back(
        grad_context, queries, key_rows, values, same_segment, log_total
    )
    grad_proj = jnp.concatenate([grad_queries, grad_keys, grad_values], axis=1)
    grad_w_qkv = matmul_tn(tokens, grad_proj)
    grad_b_qv = jnp.concatenate(
        [
            jnp.sum(grad_queries.astype(jnp.float32), axis=0),
            jnp.sum(grad_values.astype(jnp.float32), axis=0),
        ]
    )
    grad_tokens = (grad_first + matmul_nt(grad_proj, back_qkv)).astype(jnp.bfloat16)
    attn_shares = (
        lax.psum_scatter(
            grad_w_qkv.astype(jnp.bfloat16), "shard", scatter_dimension=0, tiled=True
        ).astype(jnp.float32),
        lax.psum_scatter(
            grad_b_qv.astype(jnp.bfloat16), "shard", scatter_dimension=0, tiled=True
        ).astype(jnp.float32),
        lax.psum_scatter(
            grad_w_out.astype(jnp.bfloat16), "shard", scatter_dimension=0, tiled=True
        ).astype(jnp.float32),
        lax.psum_scatter(
            grad_b_out.astype(jnp.bfloat16), "shard", scatter_dimension=0, tiled=True
        ).astype(jnp.float32),
        lax.psum_scatter(
            grad_gain_one.astype(jnp.bfloat16), "shard", scatter_dimension=0, tiled=True
        ).astype(jnp.float32),
        lax.psum_scatter(
            grad_shift_one.astype(jnp.bfloat16), "shard", scatter_dimension=0, tiled=True
        ).astype(jnp.float32),
    )
    totals = (
        lax.psum(ffn_shares[0].astype(jnp.bfloat16), "replica").astype(jnp.float32),
        lax.psum(ffn_shares[1].astype(jnp.bfloat16), "replica").astype(jnp.float32),
        lax.psum(ffn_shares[2].astype(jnp.bfloat16), "replica").astype(jnp.float32),
        lax.psum(ffn_shares[3].astype(jnp.bfloat16), "replica").astype(jnp.float32),
        lax.psum(ffn_shares[4].astype(jnp.bfloat16), "replica").astype(jnp.float32),
        lax.psum(ffn_shares[5].astype(jnp.bfloat16), "replica").astype(jnp.float32),
        lax.psum(attn_shares[0].astype(jnp.bfloat16), "replica").astype(jnp.float32),
        lax.psum(attn_shares[1].astype(jnp.bfloat16), "replica").astype(jnp.float32),
        lax.psum(attn_shares[2].astype(jnp.bfloat16), "replica").astype(jnp.float32),
        lax.psum(attn_shares[3].astype(jnp.bfloat16), "replica").astype(jnp.float32),
        lax.psum(attn_shares[4].astype(jnp.bfloat16), "replica").astype(jnp.float32),
        lax.psum(attn_shares[5].astype(jnp.bfloat16), "replica").astype(jnp.float32),
    )
    return (
        layer_out,
        grad_tokens,
        totals[6],
        totals[7],
        totals[8],
        totals[9],
        totals[10],
        totals[11],
        totals[0],
        totals[1],
        totals[2],
        totals[3],
        totals[4],
        totals[5],
    )


def on_device_direct(
    tokens,
    lengths,
    qkv_weight,
    qv_bias,
    out_weight,
    out_bias,
    first_gain,
    first_shift,
    up_weight,
    up_bias,
    down_weight,
    down_bias,
    second_gain,
    second_shift,
    cotangent,
):
    rows, model_width = tokens.shape
    replica = lax.axis_index("replica").astype(jnp.int32)
    shard = lax.axis_index("shard").astype(jnp.int32)
    z, y = shard // 2, shard % 2
    position = jnp.stack([replica, shard])
    small = (qv_bias, out_bias, first_gain, first_shift, up_bias, down_bias, second_gain, second_shift)

    def shaped(*shape, dtype=jnp.bfloat16):
        return jax.ShapeDtypeStruct(shape, dtype)

    quarter_attn = jnp.where(
        replica == 3,
        out_weight,
        lax.dynamic_slice_in_dim(qkv_weight, jnp.minimum(replica, 2) * 768, 768, axis=1),
    )
    quarter_up = lax.dynamic_index_in_dim(
        up_weight.reshape(up_weight.shape[0], SHARDS, REPLICAS, -1), replica, 2, False
    ).reshape(-1, 768)
    quarter_down = lax.dynamic_slice_in_dim(down_weight, replica * 96, 96, axis=0)
    z_attn = swap_zs(quarter_attn)
    packed = small_gather(jnp.concatenate(small), z, y)
    quarter_feed = jnp.concatenate([quarter_up, quarter_down])
    z_attn, quarter_feed = together(z_attn, quarter_feed)
    z_feed = swap_zs(quarter_feed)
    half_attn = halves_of(z_attn)
    near_attn = near_of(half_attn, cross_first(half_attn))
    far_attn = cross_second(near_attn)
    far_attn, near_attn = together(far_attn, near_attn)
    core_attn = parts_of(near_attn, far_attn, swap_cores(near_attn), swap_cores(far_attn))
    near_feed = jnp.stack(z_feed)
    far_feed = swap_y(near_feed)
    f32 = jnp.float32
    (
        w_attn,
        w_out,
        proj,
        weights,
        context,
        hidden,
        hidden_low,
        normed_one,
        inverse_one,
        table,
        keep,
    ) = kernel_call(
        attend_kernel,
        "attend",
        (
            shaped(768, 3072),
            shaped(768, 768),
            shaped(rows, 2304),
            shaped(HEADS, rows, rows, dtype=f32),
            shaped(rows, 768),
            shaped(rows, 768, dtype=f32),
            shaped(rows, 768),
            shaped(rows, 768, dtype=f32),
            shaped(rows, 1, dtype=f32),
            shaped(12, 768, dtype=f32),
            shaped(rows, 1, dtype=f32),
        ),
        [position, lengths, tokens, packed] + core_attn,
        scalars=2,
        behind=(near_feed,),
    )
    hidden_blocks = share(hidden_low)
    w_up, w_down, activated, slope, near, far = kernel_call(
        feed_kernel,
        "feed",
        (
            shaped(768, 768),
            shaped(768, 768),
            shaped(4 * rows, 768),
            shaped(4 * rows, 768, dtype=f32),
            shaped(2, rows, 768),
            shaped(2, rows, 768),
        ),
        [position, *hidden_blocks, table, near_feed, far_feed],
    )
    mine, come = collect(near, far)
    layer_out, grad_second, grad_branch, small_down = kernel_call(
        close_kernel,
        "close",
        (
            shaped(rows, 768),
            shaped(rows, 768, dtype=f32),
            shaped(rows, 768),
            shaped(3, 768, dtype=f32),
        ),
        [position, mine, come, hidden, table, keep, cotangent],
    )
    grad_blocks = share(grad_branch)
    grad_pre, near, far, grad_b_quarter = kernel_call(
        back_kernel,
        "back",
        (
            shaped(4 * rows, 768),
            shaped(2, rows, 768),
            shaped(2, rows, 768),
            shaped(1, 768, dtype=f32),
        ),
        [position, *grad_blocks, slope, w_up, w_down],
    )
    near_feed, far_feed = kernel_call(
        weight_kernel,
        "grad_feed",
        (shaped(4, 192, 768), shaped(4, 192, 768)),
        [position, activated, grad_pre, *hidden_blocks, *grad_blocks],
        [pltpu.VMEM((768, 768), jnp.bfloat16)] * 2,
    )
    come_feed = swap_y(far_feed)
    mine, come = collect(near, far)
    outs = kernel_call(
        attend_back_kernel,
        "attend_back",
        tuple(shaped(2, 4, 48, 768) for _ in range(8))
        + (
            shaped(rows, 768, dtype=f32),
            shaped(rows, 2304),
            shaped(5, 768, dtype=f32),
        ),
        [position, mine, come, grad_second, normed_one, inverse_one, table]
        + [context, proj, weights, w_out, tokens],
        [pltpu.VMEM((768, 3072), jnp.bfloat16)],
        behind=(far_feed,),
    )
    parts_attn = outs[:8]
    grad_first, grad_proj, small_attn = outs[8:]
    last_feed = plus(near_feed, come_feed)
    far, near = sum_parts(parts_attn, swap_parts(parts_attn))
    sums = jnp.concatenate(
        [
            small_attn,
            jnp.where(jnp.arange(REPLICAS)[:, None] == replica, grad_b_quarter, 0.0),
            small_down,
        ]
    )
    sums = sums + swap_z(sums, 1)
    sums = sums + swap_z(sums, 2)
    come_attn, across = together(cross_second(far), swap_core(sums))
    zs_feed = send_zs(last_feed)
    onward, stay_attn = sum_plane(near, come_attn)
    sums = sums + across
    come_attn, sums, zs_feed, grad_first = together(
        cross_first(onward), sums, zs_feed, grad_first
    )
    last_attn = sum_last(stay_attn, come_attn)
    zs_attn = send_zs(last_attn)
    reduced_feed = sum_zs(last_feed, zs_feed)
    far_feed = swap_x(reduced_feed)
    (grad_tokens,) = kernel_call(
        tokens_kernel,
        "grad_tokens",
        (shaped(rows, 768),),
        [position, grad_first, grad_proj, w_attn],
    )
    sums = sums + swap_x(sums)
    small_total = sums + swap_y(sums)
    zs_attn, far_feed, grad_tokens, small_total = together(
        zs_attn, far_feed, grad_tokens, small_total
    )
    core_feed = swap_core(jnp.stack([reduced_feed, far_feed]))
    d_up, d_down = kernel_call(
        finish_feed_kernel,
        "finish_feed",
        (shaped(96, 3072, dtype=f32), shaped(384, 768, dtype=f32)),
        [position, reduced_feed, far_feed, core_feed],
        [pltpu.VMEM((REPLICAS, 192, 768), jnp.bfloat16)],
    )
    reduced_attn = sum_zs(last_attn, zs_attn)
    far_attn = swap_x(reduced_attn)
    core_attn, d_up, d_down = together(
        swap_core(jnp.stack([reduced_attn, far_attn])), d_up, d_down
    )
    d_qkv, d_out = kernel_call(
        finish_attend_kernel,
        "finish_attend",
        (shaped(96, 2304, dtype=f32), shaped(96, 768, dtype=f32)),
        [position, reduced_attn, far_attn, core_attn],
        [pltpu.VMEM((REPLICAS, 96, 768), jnp.bfloat16)],
    )
    d_qv_bias = lax.dynamic_slice_in_dim(small_total[:2].reshape(-1), shard * 192, 192)
    mine = lax.dynamic_slice_in_dim(small_total[2:], shard * 96, 96, axis=1)
    return (
        layer_out,
        grad_tokens,
        d_qkv,
        d_qv_bias,
        d_out,
        mine[0],
        mine[1],
        mine[2],
        d_up,
        mine[3:7].reshape(-1),
        d_down,
        mine[7],
        mine[8],
        mine[9],
    )


def solution(mesh):
    shape = dict(mesh.shape)
    direct = shape["replica"] == REPLICAS and shape["shard"] == SHARDS
    placed = (
        P(("replica", "shard"), None),
        P(("replica", "shard"), None),
        P("shard", None),
        P("shard"),
        P("shard", None),
        P("shard"),
        P("shard"),
        P("shard"),
        P("shard", None),
        P("shard"),
        P("shard", None),
        P("shard"),
        P("shard"),
        P("shard"),
        P(("replica", "shard"), None),
    )
    return jax.shard_map(
        on_device_direct if direct else on_device_general,
        mesh=mesh,
        in_specs=placed,
        out_specs=(
            P(("replica", "shard"), None),
            P(("replica", "shard"), None),
            P("shard", None),
            P("shard"),
            P("shard", None),
            P("shard"),
            P("shard"),
            P("shard"),
            P("shard", None),
            P("shard"),
            P("shard", None),
            P("shard"),
            P("shard"),
            P("shard"),
        ),
        check_vma=False,
    )
```
